32 devices in a mesh: sec: 8 (over z, y), dev: 4 (over x, core).
Axes of the slice: x: 2, y: 2, z: 4, core: 2. Of those that a mesh axis runs over, the one named last changes fastest.
Arguments:
- latents: float32 [8, 4, 128, 128], P('sec', None, 'dev'), may hold values from -6 to 6
- noise: float32 [6, 8, 4, 128, 128], P(None, 'sec', None, 'dev'), may hold values from -6 to 6
- rewards: float32 [8], P('sec'), may hold values from -12 to 12
- prompt_ids: int32 [8], P('sec'), may hold values from 0 to 3
- context: bfloat16 [4, 77, 2048], replicated, may hold values from -6 to 6
- time_bias: float32 [6, 640], replicated, may hold values from -6 to 6
- gain_first: float32 [640], replicated, may hold values from 0.25 to 1.75
- gain_second: float32 [640], replicated, may hold values from 0.25 to 1.75
- gain_third: float32 [640], replicated, may hold values from 0.25 to 1.75
- w_in: bfloat16 [16, 640], P('sec', 'dev'), may hold values from -1.5 to 1.5
- w_conv: bfloat16 [5760, 640], P('sec', 'dev'), may hold values from -0.078125 to 0.078125
- w_query: bfloat16 [640, 640], P('sec', 'dev'), may hold values from -0.25 to 0.25
- w_key: bfloat16 [2048, 640], P('sec', 'dev'), may hold values from -0.125 to 0.125
- w_value: bfloat16 [2048, 640], P('sec', 'dev'), may hold values from -0.125 to 0.125
- w_attn_out: bfloat16 [640, 640], P('sec', 'dev'), may hold values from -0.25 to 0.25
- w_final: float32 [640, 16], P('sec', 'dev'), may hold values from -0.25 to 0.25
- moment_first: float32 [640, 16], P('sec', 'dev'), may hold values from -6 to 6
- moment_second: float32 [640, 16], P('sec', 'dev'), may hold values from 0.05 to 5
Outputs:
- final_latents: float32 [8, 4, 128, 128], P('sec', None, 'dev')
- new_final_weight: float32 [640, 16], P('sec', 'dev')
- moment_one: float32 [640, 16], P('sec', 'dev')
- moment_two: float32 [640, 16], P('sec', 'dev')
The draws below stay inside these ranges and needn't reach their ends.
All inputs are finite; a program needn't handle non-finite values.
Results may differ from the reference program's by a relative error of at most 0.0075.
Values may be sent and summed in bfloat16 or wider, within the bound.
No kernel may reach another device: no remote copies, remote signals or barrier semaphores. Data moves between devices by JAX's collectives and lax.ppermute only.
A program may use at most 128 MiB of HBM per device.

```python
import math
import jax
import jax.numpy as jnp
from jax import lax

C = 640
CTX = 2048
HEAD = 64
CTX_TOK = 77
FEAT = 16
LAT = 128
STEPS = 6
IMAGES = 8
NPROMPT = 4


def draw_rewards(key, part):
    position = jnp.arange(IMAGES, dtype=jnp.float32)
    scales = 1.0 + 2.0 * position / max(IMAGES - 1, 1)
    base = jax.random.normal(key, (IMAGES,), jnp.float32)
    return jnp.clip(base * scales, -12.0, 12.0)


def plant(drawn, rng, least, top_value):
    longest = drawn.shape.index(max(drawn.shape))
    spots = []
    for shift in (0, 1):
        where = [jax.random.randint(jax.random.fold_in(rng, axis), (), 0, length) for axis, length in enumerate(drawn.shape)]
        where[longest] = (where[longest] + shift) % drawn.shape[longest]
        spots.append(tuple(where))
    return drawn.at[spots[0]].set(least).at[spots[1]].set(top_value)


def shard_levels(own_key, shape, pieces, least, top_value):
    def one(dim, parts):
        heights = jax.random.uniform(jax.random.fold_in(jax.random.fold_in(own_key, 6), dim), (parts,), jnp.float32, least / len(pieces), top_value / len(pieces))
        return jnp.repeat(jnp.exp(heights), shape[dim] // parts).reshape((-1,) + (1,) * (len(shape) - dim - 1))

    loudness = one(*pieces[0])
    for cut in pieces[1:]:
        loudness = loudness * one(*cut)
    return loudness


def gaussian(stream_key, extent, width, most, pieces=(), kind=jnp.bfloat16):
    level = shard_levels(stream_key, extent, pieces, -0.22, 0.18) if pieces else 1.0
    array = jax.random.normal(stream_key, extent, jnp.float32) * width * level
    return jnp.minimum(jnp.maximum(array, -most), most).astype(kind)


def setup_inputs(seed: int = 0) -> dict:
    arg_keys = jax.random.split(jax.random.key(seed), 19)
    return {
        "latents": gaussian(arg_keys[0], (IMAGES, 4, LAT, LAT), 1.0, 6.0, ((0, 8), (2, 4)), jnp.float32),
        "noise": gaussian(arg_keys[1], (STEPS, IMAGES, 4, LAT, LAT), 1.0, 6.0, ((1, 8), (3, 4)), jnp.float32),
        "rewards": draw_rewards(jax.random.fold_in(arg_keys[18], 71), 0),
        "prompt_ids": plant(jax.random.randint(arg_keys[3], (IMAGES,), 0, NPROMPT), jax.random.fold_in(arg_keys[3], 1), 0, NPROMPT - 1).astype(jnp.int32),
        "context": gaussian(arg_keys[4], (NPROMPT, CTX_TOK, CTX), 1.0, 6.0),
        "time_bias": gaussian(arg_keys[5], (STEPS, C), 1.0, 6.0, (), jnp.float32),
        "gain_first": jnp.clip(1.0 + 0.15 * jax.random.normal(arg_keys[6], (C,), jnp.float32), 0.25, 1.75),
        "gain_second": jnp.clip(1.0 + 0.15 * jax.random.normal(arg_keys[7], (C,), jnp.float32), 0.25, 1.75),
        "gain_third": jnp.clip(1.0 + 0.15 * jax.random.normal(arg_keys[8], (C,), jnp.float32), 0.25, 1.75),
        "w_in": gaussian(arg_keys[9], (FEAT, C), FEAT ** -0.5, 1.5, ((0, 8), (1, 4))),
        "w_conv": gaussian(arg_keys[10], (9 * C, C), (9 * C) ** -0.5, 0.078125, ((0, 8), (1, 4))),
        "w_query": gaussian(arg_keys[11], (C, C), C ** -0.5, 0.25, ((0, 8), (1, 4))),
        "w_key": gaussian(arg_keys[12], (CTX, C), CTX ** -0.5, 0.125, ((0, 8), (1, 4))),
        "w_value": gaussian(arg_keys[13], (CTX, C), CTX ** -0.5, 0.125, ((0, 8), (1, 4))),
        "w_attn_out": gaussian(arg_keys[14], (C, C), C ** -0.5, 0.25, ((0, 8), (1, 4))),
        "w_final": gaussian(arg_keys[15], (C, FEAT), C ** -0.5, 0.25, ((0, 8), (1, 4)), jnp.float32),
        "moment_first": gaussian(arg_keys[16], (C, FEAT), 1.0, 6.0, ((0, 8), (1, 4)), jnp.float32),
        "moment_second": jnp.clip(jnp.exp(math.log(5.0) - 4.6051702 * jax.random.uniform(arg_keys[17], (C, FEAT), jnp.float32) ** shard_levels(arg_keys[17], (C, FEAT), ((0, 8), (1, 4)), -0.2, 0.2)), 0.05, 5.0),
    }


alpha_bars = (0.1, 0.15, 0.21, 0.28, 0.36, 0.45, 0.55)
norm_eps = 1e-06
learn_rate = 0.001

def plan(step_index):
    current = alpha_bars[step_index]
    following = alpha_bars[step_index + 1]
    sigma = math.sqrt((1.0 - following) / (1.0 - current)) * math.sqrt(1.0 - current / following)
    scale = math.sqrt(following / current)
    beta = math.sqrt(1.0 - following - sigma * sigma) - scale * math.sqrt(1.0 - current)
    return (scale, beta, sigma)

def rms_scale(values, gain):
    mean_square = lax.optimization_barrier(jnp.mean(values * values, axis=-1, keepdims=True))
    return values * lax.rsqrt(mean_square + norm_eps) * gain

def to_tokens(latent):
    batch_size, latent_chans, height, breadth = latent.shape
    blocks = latent.reshape(batch_size, latent_chans, height // 2, 2, breadth // 2, 2)
    return blocks.transpose(0, 2, 4, 1, 3, 5).reshape(batch_size, height // 2, breadth // 2, latent_chans * 4)

def from_tokens(tokens):
    batch_size, rows_here, cols_here, feature_count = tokens.shape
    blocks = tokens.reshape(batch_size, rows_here, cols_here, feature_count // 4, 2, 2)
    return blocks.transpose(0, 3, 1, 4, 2, 5).reshape(batch_size, feature_count // 4, 2 * rows_here, 2 * cols_here)

def denoise(patches, prompt_keys, prompt_values, step_bias, weights, gains):
    w_first, w_conv, w_query, w_attn_out, final_weight = weights
    batch_size, rows_here, cols_here, feature_count = patches.shape
    channels = w_first.shape[1]
    head_count = channels // HEAD
    flat_rows = batch_size * rows_here * cols_here
    hidden_in = jnp.dot(patches.astype(jnp.bfloat16).reshape(flat_rows, feature_count), w_first, preferred_element_type=jnp.float32) + step_bias
    activated = jax.nn.silu(rms_scale(hidden_in, gains[0])).astype(jnp.bfloat16).reshape(batch_size, rows_here, cols_here, channels)
    padded = jnp.pad(activated, ((0, 0), (1, 1), (1, 1), (0, 0)))
    columns = jnp.concatenate([padded[:, row_off:row_off + rows_here, col_off:col_off + cols_here] for row_off in range(3) for col_off in range(3)], axis=-1)
    mixed_rows = hidden_in + jnp.dot(columns.reshape(flat_rows, 9 * channels), w_conv, preferred_element_type=jnp.float32)
    normed = rms_scale(mixed_rows, gains[1]).astype(jnp.bfloat16)
    queries = jnp.dot(normed, w_query, preferred_element_type=jnp.float32).astype(jnp.bfloat16)
    queries = queries.reshape(batch_size, rows_here * cols_here, head_count, HEAD)
    key_heads = prompt_keys.reshape(batch_size, -1, head_count, HEAD)
    value_heads = prompt_values.reshape(batch_size, -1, head_count, HEAD)
    scores = jnp.einsum('bthd,bkhd->bthk', queries.astype(jnp.float32), key_heads.astype(jnp.float32)) / math.sqrt(HEAD)
    exponent = jnp.exp(scores)
    probabilities = (exponent / lax.optimization_barrier(jnp.sum(exponent, axis=-1, keepdims=True))).astype(jnp.bfloat16)
    attended = jnp.einsum('bthk,bkhd->bthd', probabilities.astype(jnp.float32), value_heads.astype(jnp.float32)).astype(jnp.bfloat16)
    output_rows = mixed_rows + jnp.dot(attended.reshape(flat_rows, channels), w_attn_out, preferred_element_type=jnp.float32)
    final_act = jax.nn.silu(rms_scale(output_rows, gains[2])).astype(jnp.bfloat16)
    predicted = jnp.dot(final_act, final_weight, preferred_element_type=jnp.float32)
    return (predicted.reshape(batch_size, rows_here, cols_here, feature_count), final_act)

def advantages(onehot, rewards, counts, sums, squares):
    safe_count = jnp.maximum(counts, 1.0)
    means = sums / safe_count
    spreads = jnp.sqrt(jnp.maximum(squares / safe_count - means * means, 1.0))
    own_mean = lax.optimization_barrier(jnp.sum(onehot * means[None, :], axis=1))
    own_spread = lax.optimization_barrier(jnp.sum(onehot * spreads[None, :], axis=1))
    return (rewards - own_mean) / own_spread

def reference(latents, noise, rewards, prompt_ids, context, time_bias, gain_first, gain_second, gain_third, w_in, w_conv, w_query, w_key, w_value, w_attn_out, w_final, moment_first, moment_second):
    catalog = jnp.arange(NPROMPT, dtype=jnp.int32)
    onehot = (prompt_ids[:, None] == catalog[None, :]).astype(jnp.float32)
    counts = lax.optimization_barrier(jnp.sum(onehot, axis=0))
    sums = lax.optimization_barrier(jnp.sum(onehot * rewards[:, None], axis=0))
    squares = lax.optimization_barrier(jnp.sum(onehot * (rewards * rewards)[:, None], axis=0))
    advantage = advantages(onehot, rewards, counts, sums, squares)
    flat_context = context.reshape(NPROMPT * CTX_TOK, CTX)
    all_keys = jnp.dot(flat_context, w_key, preferred_element_type=jnp.float32).astype(jnp.bfloat16).reshape(NPROMPT, CTX_TOK, C)
    all_values = jnp.dot(flat_context, w_value, preferred_element_type=jnp.float32).astype(jnp.bfloat16).reshape(NPROMPT, CTX_TOK, C)
    final_weight = w_final.astype(jnp.bfloat16)
    weights = (w_in, w_conv, w_query, w_attn_out, final_weight)
    gains = (gain_first, gain_second, gain_third)

    def one_image(item):
        latent, noise_rows, image_prompt, image_adv = item
        latent = latent[None]
        own_keys = lax.dynamic_index_in_dim(all_keys, image_prompt.astype(jnp.int32), 0, keepdims=True)
        own_values = lax.dynamic_index_in_dim(all_values, image_prompt.astype(jnp.int32), 0, keepdims=True)
        gradient = jnp.zeros((C, FEAT), jnp.float32)
        for step_index in range(STEPS):
            scale, beta, sigma = plan(step_index)
            patches = to_tokens(latent)
            predicted, final_act = denoise(patches, own_keys, own_values, time_bias[step_index], weights, gains)
            noise_now = noise_rows[step_index][None]
            noise_patch = to_tokens(noise_now).reshape(-1, FEAT)
            weighted = noise_patch * (image_adv * (beta / sigma))
            gradient = gradient + jnp.dot(final_act.astype(jnp.float32).T, weighted, precision=lax.Precision.HIGHEST)
            latent = scale * latent + beta * from_tokens(predicted) + sigma * noise_now
        return (latent[0], gradient)
    finals, grads = lax.map(one_image, (latents, noise.transpose(1, 0, 2, 3, 4), prompt_ids, advantage))
    grad_total = -lax.optimization_barrier(jnp.sum(grads, axis=0)) / IMAGES
    moment_one = 0.9 * moment_first + 0.1 * grad_total
    moment_two = 0.999 * moment_second + 0.001 * grad_total * grad_total
    new_weight = w_final - learn_rate * moment_one / (jnp.sqrt(moment_two) + 1e-08)
    return (finals, new_weight, moment_one, moment_two)
```

```python
import functools
import math

import jax
import jax.numpy as jnp
from jax import lax
from jax.experimental import pallas as pl
from jax.experimental.pallas import tpu as pltpu
from jax.sharding import PartitionSpec as P

HEAD = 64
STEPS = 6
GROUP = 3
CHUNK_ROWS = 4

alpha_bars = (0.1, 0.15, 0.21, 0.28, 0.36, 0.45, 0.55)
norm_eps = 1e-06
learn_rate = 0.001


def plan(step_index):
    current = alpha_bars[step_index]
    following = alpha_bars[step_index + 1]
    sigma = math.sqrt((1.0 - following) / (1.0 - current)) * math.sqrt(1.0 - current / following)
    scale = math.sqrt(following / current)
    beta = math.sqrt(1.0 - following - sigma * sigma) - scale * math.sqrt(1.0 - current)
    return (scale, beta, sigma)


def swap(value, axis, mask):
    size = lax.axis_size(axis)
    return lax.ppermute(value, axis, [(i, i ^ mask) for i in range(size)])


def bit_of(axis, mask):
    return (lax.axis_index(axis) & mask) != 0


def doubled_gather(value, axis):
    mask = 1
    while mask < lax.axis_size(axis):
        other = swap(value, axis, mask)
        upper = bit_of(axis, mask)
        value = jnp.concatenate(
            [jnp.where(upper, other, value), jnp.where(upper, value, other)], axis=0
        )
        mask *= 2
    return value


def halved_sum(value, axis):
    mask = lax.axis_size(axis) // 2
    while mask >= 1:
        half = value.shape[0] // 2
        upper = bit_of(axis, mask)
        kept = jnp.where(upper, value[half:], value[:half])
        sent = jnp.where(upper, value[:half], value[half:])
        value = kept + swap(sent, axis, mask)
        mask //= 2
    return value


def with_halo(shard, axis, dim, width):
    size, length = (lax.axis_size(axis), shard.shape[dim])
    up = [(i, i + 1) for i in range(size - 1)]
    down = [(j, i) for i, j in up]
    last = lax.slice_in_dim(shard, length - width, length, axis=dim)
    first = lax.slice_in_dim(shard, 0, width, axis=dim)
    before = lax.ppermute(last, axis, up)
    after = lax.ppermute(first, axis, down)
    return jnp.concatenate([before, shard, after], axis=dim)


def to_tokens(latent):
    lead = latent.shape[:-3]
    chans, height, breadth = latent.shape[-3:]
    n = len(lead)
    blocks = latent.reshape(lead + (chans, height // 2, 2, breadth // 2, 2))
    order = tuple(range(n)) + (n + 1, n + 3, n, n + 2, n + 4)
    return blocks.transpose(order).reshape(lead + (height * breadth // 4, chans * 4))


def from_tokens(tokens, rows, cols):
    feats = tokens.shape[-1]
    blocks = tokens.reshape(rows, cols, feats // 4, 2, 2)
    return blocks.transpose(2, 0, 3, 1, 4).reshape(feats // 4, 2 * rows, 2 * cols)


def rms_scale(values, gain):
    mean_square = jnp.mean(values * values, axis=-1, keepdims=True)
    return values * lax.rsqrt(mean_square + norm_eps) * gain


def silu(values):
    return 0.5 * values * (1.0 + jnp.tanh(0.5 * values))


def row_chunks(first, last, width):
    out = []
    while first < last:
        out.append((first, min(width, last - first)))
        first += width
    return out


def steps_kernel(
    factors,
    rows,
    cols,
    counts,
    flags,
    packed,
    x_in,
    noise,
    noise_grad,
    key_blocks,
    value_blocks,
    bias,
    gains,
    w_in,
    w_final,
    x_out,
    grad_out,
    w_conv,
    w_query,
    w_attn,
    hidden,
    columns,
    state,
    acts,
    sems,
):
    group = len(factors)
    chans = w_in.shape[1]
    parts = packed.shape[0]
    copies = []
    offset = 0
    for which, (count, ref) in enumerate(zip(counts, (w_conv, w_query, w_attn))):
        copies.append([])
        for part in range(parts):
            copy = pltpu.make_async_copy(
                packed.at[part, pl.ds(offset, count)],
                ref.at[pl.ds(part * count, count)],
                sems.at[which, part],
            )
            copy.start()
            copies[-1].append(copy)
        offset += count
    state[...] = x_in[...]
    pairs = key_blocks.shape[0]
    wide = 2 * HEAD
    for step, (scale, beta, sigma) in enumerate(factors):
        halo = group - step
        spans = (
            [(group - halo, halo, 0)]
            + [(r, n, None) for r, n in row_chunks(group, group + rows, CHUNK_ROWS)]
            + [(group + rows, halo, 1)]
        )
        for row, count, edge in spans:
            span = pl.ds(row * cols, count * cols)
            before_norm = (
                jnp.dot(
                    state[span, :].astype(jnp.bfloat16),
                    w_in[...],
                    preferred_element_type=jnp.float32,
                )
                + bias[step : step + 1, :]
            )
            hidden[span, :] = before_norm
            act = silu(rms_scale(before_norm, gains[0:1, :]))
            if edge is not None:
                act = act * flags[edge]
            size = count * cols
            col = lax.rem(lax.broadcasted_iota(jnp.int32, (size, 1), 0), cols)
            left = jnp.where(col == 0, 0.0, pltpu.roll(act, 1, 0))
            right = jnp.where(col == cols - 1, 0.0, pltpu.roll(act, size - 1, 0))
            columns[span, 0:chans] = left.astype(jnp.bfloat16)
            columns[span, chans : 2 * chans] = act.astype(jnp.bfloat16)
            columns[span, 2 * chans : 3 * chans] = right.astype(jnp.bfloat16)
        if step == 0:
            for copy in copies[0]:
                copy.wait()
        grown = halo - 1
        for number, (row, count) in enumerate(
            row_chunks(group - grown, group + rows + grown, CHUNK_ROWS)
        ):
            span = pl.ds(row * cols, count * cols)
            mixed = hidden[span, :]
            for dr in range(3):
                mixed = mixed + jnp.dot(
                    columns[pl.ds((row + dr - 1) * cols, count * cols), :],
                    w_conv[dr * 3 * chans : (dr + 1) * 3 * chans, :],
                    preferred_element_type=jnp.float32,
                )
            if step == 0 and number == 0:
                for copy in copies[1] + copies[2]:
                    copy.wait()
            normed = rms_scale(mixed, gains[1:2, :]).astype(jnp.bfloat16)
            queries = jnp.dot(normed, w_query[...], preferred_element_type=jnp.float32).astype(
                jnp.bfloat16
            )
            heads = []
            for pair in range(pairs):
                scores = jnp.dot(
                    queries[:, pair * wide : (pair + 1) * wide],
                    key_blocks[pair],
                    preferred_element_type=jnp.float32,
                )
                sums = jnp.dot(
                    jnp.exp(scores).astype(jnp.bfloat16),
                    value_blocks[pair],
                    preferred_element_type=jnp.float32,
                )
                heads.append((sums[:, :wide] / sums[:, wide:]).astype(jnp.bfloat16))
            attended = jnp.concatenate(heads, axis=1)
            output = mixed + jnp.dot(attended, w_attn[...], preferred_element_type=jnp.float32)
            act = silu(rms_scale(output, gains[2:3, :])).astype(jnp.bfloat16)
            predicted = jnp.dot(act, w_final[...], preferred_element_type=jnp.float32)
            noise_span = pl.ds((row - 1) * cols, count * cols)
            state[span, :] = (
                scale * state[span, :] + beta * predicted + sigma * noise[step, noise_span, :]
            )
            low, high = max(row, group), min(row + count, group + rows)
            if low < high:
                acts[pl.ds((low - group) * cols, (high - low) * cols), :] = act[
                    (low - row) * cols : (high - row) * cols, :
                ]
        share = jnp.dot(noise_grad[step], acts[...], preferred_element_type=jnp.float32)
        if step == 0:
            grad_out[...] = share
        else:
            grad_out[...] += share
    x_out[...] = state[pl.ds(group * cols, rows * cols), :]


def run_steps(first, rows, cols, counts, flags, packed, x, noise, noise_grad, rest, bias):
    factors = tuple(plan(first + k) for k in range(GROUP))
    key_blocks, value_blocks, gains, w_in, w_final = rest
    feats, chans = w_in.shape
    parts = packed.shape[0]
    tall = (rows + 2 * GROUP) * cols
    vmem = pl.BlockSpec(memory_space=pltpu.VMEM)
    token_rows = sum(rows + 2 * k for k in range(GROUP)) * cols
    return pl.pallas_call(
        functools.partial(steps_kernel, factors, rows, cols, counts),
        out_shape=(
            jax.ShapeDtypeStruct((rows * cols, feats), jnp.float32),
            jax.ShapeDtypeStruct((noise_grad.shape[1], chans), jnp.float32),
        ),
        in_specs=[pl.BlockSpec(memory_space=pltpu.SMEM), pl.BlockSpec(memory_space=pl.ANY)]
        + [vmem] * 9,
        out_specs=(vmem, vmem),
        scratch_shapes=[
            pltpu.VMEM((9 * chans, chans), jnp.bfloat16),
            pltpu.VMEM((chans, chans), jnp.bfloat16),
            pltpu.VMEM((chans, chans), jnp.bfloat16),
            pltpu.VMEM((tall, chans), jnp.float32),
            pltpu.VMEM((tall, 3 * chans), jnp.bfloat16),
            pltpu.VMEM((tall, feats), jnp.float32),
            pltpu.VMEM((rows * cols, chans), jnp.bfloat16),
            pltpu.SemaphoreType.DMA((3, parts)),
        ],
        compiler_params=pltpu.CompilerParams(vmem_limit_bytes=52 * 2**20),
        cost_estimate=pl.CostEstimate(
            flops=2 * token_rows * chans * chans * 12,
            bytes_accessed=12 * chans * chans * 2,
            transcendentals=4 * token_rows * chans,
        ),
    )(
        flags,
        packed,
        x,
        noise,
        noise_grad,
        key_blocks,
        value_blocks,
        bias,
        gains,
        w_in,
        w_final,
    )


def advantages(onehot, own, rewards, own_reward):
    counts = jnp.sum(onehot, axis=0)
    sums = jnp.sum(onehot * rewards[:, None], axis=0)
    squares = jnp.sum(onehot * (rewards * rewards)[:, None], axis=0)
    safe_count = jnp.maximum(counts, 1.0)
    means = sums / safe_count
    spreads = jnp.sqrt(jnp.maximum(squares / safe_count - means * means, 1.0))
    own_mean = jnp.sum(own * means)
    own_spread = jnp.sum(own * spreads)
    return (own_reward - own_mean) / own_spread


def per_device(
    latents,
    noise,
    rewards,
    prompt_ids,
    context,
    time_bias,
    gain_first,
    gain_second,
    gain_third,
    w_in,
    w_conv,
    w_query,
    w_key,
    w_value,
    w_attn_out,
    w_final,
    moment_first,
    moment_second,
):
    sec_count = lax.axis_size("sec")
    dev_count = lax.axis_size("dev")
    prompt_count, context_tokens, _ = context.shape
    assert latents.shape[0] == 1
    col_piece = w_conv.shape[1]
    chans = col_piece * dev_count
    feats = w_in.shape[0] * sec_count
    rows, cols = latents.shape[2] // 2, latents.shape[3] // 2

    pieces = [
        w_conv,
        w_query,
        w_attn_out,
        w_in,
        w_final.astype(jnp.bfloat16).reshape(-1, col_piece),
    ]
    counts = [piece.shape[0] for piece in pieces]
    used = sum(counts)
    unit = 16 * dev_count
    padded = -(-used // unit) * unit
    pieces.append(jnp.zeros((padded - used, col_piece), jnp.bfloat16))
    block = jnp.concatenate(pieces, axis=0)
    block = lax.all_to_all(block, "dev", split_axis=0, concat_axis=1, tiled=True)
    packed = lax.all_gather(block, ("sec", "dev"), axis=0, tiled=True)
    packed = packed.reshape(sec_count, padded, chans)
    at = counts[0] + counts[1] + counts[2]
    in_full = packed[:, at : at + counts[3]].reshape(feats, chans)
    at += counts[3]
    final_full = (
        packed[:, at : at + counts[4]]
        .reshape(sec_count, counts[4], dev_count, col_piece)
        .transpose(0, 2, 1, 3)
        .reshape(sec_count, dev_count, chans // sec_count, feats // dev_count)
        .transpose(0, 2, 1, 3)
        .reshape(chans, feats)
    )
    big = counts[:3]
    if any(count % 16 for count in big):
        packed = jnp.concatenate(
            [
                packed[:, sum(big[:k]) : sum(big[: k + 1])].reshape(-1, chans)
                for k in range(3)
            ],
            axis=0,
        )[None]
        big = [count * sec_count for count in big]

    both = jnp.stack([rewards, prompt_ids.astype(jnp.float32)], axis=1)
    both = doubled_gather(both, "sec")
    all_rewards = both[:, 0]
    catalog = jnp.arange(prompt_count, dtype=jnp.int32)
    onehot = (both[:, 1].astype(jnp.int32)[:, None] == catalog[None, :]).astype(jnp.float32)
    own = (prompt_ids == catalog).astype(jnp.float32)
    advantage = advantages(onehot, own, all_rewards, rewards[0])

    key_rows = w_key.shape[0]
    tokens_up = -(-context_tokens // 16) * 16
    own_context = lax.dynamic_slice_in_dim(
        context, lax.axis_index("sec") * key_rows, key_rows, axis=2
    )
    own_context = jnp.pad(own_context, ((0, 0), (0, tokens_up - context_tokens), (0, 0)))
    partial = jnp.dot(
        own_context.reshape(prompt_count * tokens_up, key_rows),
        jnp.concatenate([w_key, w_value], axis=1),
        preferred_element_type=jnp.float32,
    ).reshape(prompt_count, tokens_up, 2 * col_piece)
    wanted = jnp.einsum(
        "ip,ptc->itc", onehot, partial, precision=lax.Precision.HIGHEST
    )
    own_part = halved_sum(wanted, "sec").astype(jnp.bfloat16)
    whole = doubled_gather(own_part, "dev").reshape(dev_count, tokens_up, 2, col_piece)
    whole = whole.transpose(2, 1, 0, 3).reshape(2, tokens_up, chans)
    lane = 2 * HEAD
    pairs = chans // lane
    valid = jnp.arange(tokens_up)[None, :, None] < context_tokens
    by_pair = jnp.where(valid, whole, 0).reshape(2, tokens_up, pairs, 2, HEAD)
    by_pair = jnp.pad(by_pair, ((0, 0), (0, lane - tokens_up), (0, 0), (0, 0), (0, 0)))
    eye = jnp.eye(2, dtype=jnp.bfloat16)
    key_blocks = (
        (by_pair[0] * (1.0 / math.sqrt(HEAD))).astype(jnp.bfloat16).transpose(1, 2, 3, 0)[
            :, :, :, None, :
        ]
        * eye[None, :, None, :, None]
    ).reshape(pairs, lane, 2 * lane)
    value_blocks = (
        by_pair[1].transpose(1, 2, 0, 3)[:, :, :, None, :] * eye[None, :, None, :, None]
    ).reshape(pairs, 2 * lane, lane)
    inside = (jnp.arange(lane) < context_tokens).astype(jnp.bfloat16)
    ones = jnp.broadcast_to(
        inside[None, :, None, None] * eye[:, None, :, None], (2, lane, 2, HEAD)
    ).reshape(1, 2 * lane, lane)
    value_blocks = jnp.concatenate(
        [value_blocks, jnp.broadcast_to(ones, value_blocks.shape)], axis=2
    )

    position = lax.axis_index("dev")
    flags = jnp.stack([position > 0, position < dev_count - 1]).astype(jnp.float32)
    x = to_tokens(with_halo(latents, "dev", 2, 2 * GROUP)[0])
    noise_wide = to_tokens(with_halo(noise, "dev", 3, 2 * (GROUP - 1))[:, 0])
    own_noise = noise_wide[:, (GROUP - 1) * cols : (GROUP - 1 + rows) * cols]
    ratios = jnp.array([plan(k)[1] / plan(k)[2] for k in range(STEPS)], jnp.float32)
    weighted = own_noise.transpose(0, 2, 1) * ratios[:, None, None]
    upper = lax.reduce_precision(weighted, 8, 7)
    noise_grad = jnp.concatenate([upper, weighted - upper], axis=1).astype(jnp.bfloat16)

    gains = jnp.stack([gain_first, gain_second, gain_third])
    rest = (key_blocks, value_blocks, gains, in_full, final_full)
    gradient = jnp.zeros((2 * feats, chans), jnp.float32)
    for first in range(0, STEPS, GROUP):
        if first:
            x = with_halo(x, "dev", 0, GROUP * cols)
        part = slice(first, first + GROUP)
        x, share = run_steps(
            first,
            rows,
            cols,
            big,
            flags,
            packed,
            x,
            noise_wide[part],
            noise_grad[part],
            rest,
            time_bias[part],
        )
        gradient = gradient + share
    latent = from_tokens(x, rows, cols)[None]

    gradient = (gradient[:feats] + gradient[feats:]) * advantage
    row_piece = chans // sec_count
    arranged = gradient.reshape(dev_count, feats // dev_count, sec_count, row_piece)
    arranged = arranged.transpose(2, 0, 1, 3)
    grad_shard = halved_sum(halved_sum(arranged, "sec")[0], "dev")[0].T
    grad_shard = -grad_shard / sec_count
    moment_one = 0.9 * moment_first + 0.1 * grad_shard
    moment_two = 0.999 * moment_second + 0.001 * grad_shard * grad_shard
    new_weight = w_final - learn_rate * moment_one / (jnp.sqrt(moment_two) + 1e-08)
    return (latent, new_weight, moment_one, moment_two)


def solution(mesh):
    weight = P("sec", "dev")
    placed = (
        (P("sec", None, "dev", None), P(None, "sec", None, "dev", None), P("sec"), P("sec"))
        + (P(),) * 5
        + (weight,) * 9
    )
    return jax.shard_map(
        per_device,
        mesh=mesh,
        in_specs=placed,
        out_specs=(P("sec", None, "dev", None), weight, weight, weight),
        check_vma=False,
    )
```

```python
import functools
import math

import jax
import jax.numpy as jnp
from jax import lax
from jax.experimental import pallas as pl
from jax.experimental.pallas import tpu as pltpu
from jax.sharding import PartitionSpec as P

HEAD = 64
STEPS = 6
GROUP = 3
HALO = 4
CHUNK_ROWS = 4

alpha_bars = (0.1, 0.15, 0.21, 0.28, 0.36, 0.45, 0.55)
norm_eps = 1e-06
learn_rate = 0.001


def plan(step_index):
    current = alpha_bars[step_index]
    following = alpha_bars[step_index + 1]
    sigma = math.sqrt((1.0 - following) / (1.0 - current)) * math.sqrt(1.0 - current / following)
    scale = math.sqrt(following / current)
    beta = math.sqrt(1.0 - following - sigma * sigma) - scale * math.sqrt(1.0 - current)
    return (scale, beta, sigma)


def swap(value, axis, mask):
    size = lax.axis_size(axis)
    return lax.ppermute(value, axis, [(i, i ^ mask) for i in range(size)])


def bit_of(axis, mask):
    return (lax.axis_index(axis) & mask) != 0


def doubled_gather(value, axis):
    mask = 1
    while mask < lax.axis_size(axis):
        other = swap(value, axis, mask)
        upper = bit_of(axis, mask)
        value = jnp.concatenate(
            [jnp.where(upper, other, value), jnp.where(upper, value, other)], axis=0
        )
        mask *= 2
    return value


def halved_sum(value, axis, link=jnp.float32):
    mask = lax.axis_size(axis) // 2
    while mask >= 1:
        half = value.shape[0] // 2
        upper = bit_of(axis, mask)
        kept = jnp.where(upper, value[half:], value[:half])
        sent = jnp.where(upper, value[:half], value[half:])
        value = kept + swap(sent.astype(link), axis, mask).astype(value.dtype)
        mask //= 2
    return value


def with_halo(shard, axis, dim, width):
    size, length = (lax.axis_size(axis), shard.shape[dim])
    up = [(i, i + 1) for i in range(size - 1)]
    down = [(j, i) for i, j in up]
    last = lax.slice_in_dim(shard, length - width, length, axis=dim)
    first = lax.slice_in_dim(shard, 0, width, axis=dim)
    before = lax.ppermute(last, axis, up)
    after = lax.ppermute(first, axis, down)
    return jnp.concatenate([before, shard, after], axis=dim)


def lane_order(breadth):
    half = breadth // 2
    lane = jnp.arange(breadth)
    return (lane[:, None] == (2 * (lane % half) + lane // half)[None, :]).astype(jnp.float32)


def to_tokens(latent):
    count, chans, height, breadth = latent.shape
    split = jnp.dot(latent, lane_order(breadth), precision=lax.Precision.HIGHEST)
    blocks = split.reshape(count, chans, height // 2, 2, 2, breadth // 2)
    return blocks.transpose(0, 1, 3, 4, 2, 5).reshape(
        count, chans * 4, height * breadth // 4
    )


def from_tokens(tokens, rows, cols):
    feats = tokens.shape[0]
    blocks = tokens.reshape(feats // 4, 2, 2, rows, cols).transpose(0, 3, 1, 2, 4)
    return jnp.dot(
        blocks.reshape(feats // 4, 2 * rows, 2 * cols),
        lane_order(2 * cols).T,
        precision=lax.Precision.HIGHEST,
    )


def rms_scale(values, gain):
    mean_square = jnp.mean(values * values, axis=-1, keepdims=True)
    return values * lax.rsqrt(mean_square + norm_eps) * gain


def silu(values):
    return 0.5 * values * (1.0 + jnp.tanh(0.5 * values))


def steps_kernel(
    rows,
    cols,
    counts,
    flags,
    factors,
    packed,
    x_in,
    noise,
    key_blocks,
    value_blocks,
    bias,
    gains,
    w_in,
    w_final,
    x_out,
    grad_out,
    w_conv,
    w_query,
    w_attn,
    hidden,
    columns,
    state,
    sems,
):
    group = bias.shape[0]
    feats, chans = w_in.shape
    parts = packed.shape[0]
    copies = []
    offset = 0
    for which, (count, ref) in enumerate(zip(counts, (w_conv, w_query, w_attn))):
        copies.append([])
        for part in range(parts):
            copy = pltpu.make_async_copy(
                packed.at[part, pl.ds(offset, count)],
                ref.at[pl.ds(part * count, count)],
                sems.at[which, part],
            )
            copy.start()
            copies[-1].append(copy)
        offset += count
    state[...] = x_in[...]
    grad_out[...] = jnp.zeros_like(grad_out)
    pairs = key_blocks.shape[0]
    wide = 2 * HEAD
    size = CHUNK_ROWS * cols
    token = lax.broadcasted_iota(jnp.int32, (size, 1), 0)
    lane_token = lax.broadcasted_iota(jnp.int32, (1, size), 1)
    col = lax.rem(token, cols)

    def activate(step, chunk):
        start = pl.multiple_of(chunk * size, size)
        span = pl.ds(start, size)
        before_norm = (
            lax.dot_general(
                state[:, span].astype(jnp.bfloat16),
                w_in[...],
                (((0,), (0,)), ((), ())),
                preferred_element_type=jnp.float32,
            )
            + bias[pl.ds(step, 1), :]
        )
        hidden[span, :] = before_norm
        act = silu(rms_scale(before_norm, gains[0:1, :]))
        inside = jnp.where(
            start + token < HALO * cols,
            flags[0],
            jnp.where(start + token >= (HALO + rows) * cols, flags[1], 1.0),
        )
        act = act * inside
        left = jnp.where(col == 0, 0.0, pltpu.roll(act, 1, 0))
        right = jnp.where(col == cols - 1, 0.0, pltpu.roll(act, size - 1, 0))
        columns[span, 0:chans] = left.astype(jnp.bfloat16)
        columns[span, chans : 2 * chans] = act.astype(jnp.bfloat16)
        columns[span, 2 * chans : 3 * chans] = right.astype(jnp.bfloat16)

    def convolve(start):
        mixed = hidden[pl.ds(start, size), :]
        for dr in range(3):
            mixed = mixed + jnp.dot(
                columns[pl.ds(start + (dr - 1) * cols, size), :],
                w_conv[dr * 3 * chans : (dr + 1) * 3 * chans, :],
                preferred_element_type=jnp.float32,
            )
        return mixed

    def finish(step, start, mixed):
        normed = rms_scale(mixed, gains[1:2, :]).astype(jnp.bfloat16)
        queries = jnp.dot(normed, w_query[...], preferred_element_type=jnp.float32).astype(
            jnp.bfloat16
        )
        heads = []
        for pair in range(pairs):
            scores = jnp.dot(
                queries[:, pair * wide : (pair + 1) * wide],
                key_blocks[pair],
                preferred_element_type=jnp.float32,
            )
            sums = jnp.dot(
                jnp.exp(scores).astype(jnp.bfloat16),
                value_blocks[pair],
                preferred_element_type=jnp.float32,
            )
            heads.append((sums[:, :wide] / sums[:, wide:]).astype(jnp.bfloat16))
        attended = jnp.concatenate(heads, axis=1)
        output = mixed + jnp.dot(attended, w_attn[...], preferred_element_type=jnp.float32)
        act = silu(rms_scale(output, gains[2:3, :])).astype(jnp.bfloat16)
        predicted = jnp.dot(act, w_final[...], preferred_element_type=jnp.float32)
        span = pl.ds(start, size)
        noise_now = noise[step, :, span]
        state[:, span] = (
            factors[step, 0] * state[:, span]
            + factors[step, 1] * predicted.T
            + factors[step, 2] * noise_now
        )
        place = start + lane_token
        own = (place >= HALO * cols) & (place < (HALO + rows) * cols)
        weights = jnp.where(own, noise_now, 0.0)
        upper = weights.astype(jnp.bfloat16)
        lower = (weights - upper.astype(jnp.float32)).astype(jnp.bfloat16)
        share = jnp.dot(
            jnp.concatenate([upper, lower], axis=0), act, preferred_element_type=jnp.float32
        )
        grad_out[...] += factors[step, 3] * (share[:feats] + share[feats:])

    chunks = state.shape[1] // size

    def one_step(step, carry):
        def fill(chunk, carry):
            activate(step, chunk)
            return carry

        lax.fori_loop(0, chunks, fill, 0)
        last = step == group - 1
        base = jnp.where(last, HALO, HALO // 2) * cols
        count = jnp.where(last, chunks - 2, chunks - 1)

        @pl.when(step == 0)
        def _():
            for some in copies:
                for copy in some:
                    copy.wait()

        def place(number):
            return pl.multiple_of(base + number * size, 2 * cols)

        def body(number, mixed):
            following = convolve(place(number))
            finish(step, place(number - 1), mixed)
            return following

        mixed = lax.fori_loop(1, count, body, convolve(place(0)))
        finish(step, place(count - 1), mixed)
        return carry

    lax.fori_loop(0, group, one_step, 0)
    x_out[...] = state[:, HALO * cols : (HALO + rows) * cols]


def run_steps(rows, cols, counts, flags, factors, packed, x, noise, rest, bias):
    key_blocks, value_blocks, gains, w_in, w_final = rest
    feats, chans = w_in.shape
    parts = packed.shape[0]
    tall = (rows + 2 * HALO) * cols
    vmem = pl.BlockSpec(memory_space=pltpu.VMEM)
    smem = pl.BlockSpec(memory_space=pltpu.SMEM)
    token_rows = sum(rows + 2 * k for k in range(GROUP)) * cols
    return pl.pallas_call(
        functools.partial(steps_kernel, rows, cols, counts),
        out_shape=(
            jax.ShapeDtypeStruct((feats, rows * cols), jnp.float32),
            jax.ShapeDtypeStruct((feats, chans), jnp.float32),
        ),
        in_specs=[smem, smem, pl.BlockSpec(memory_space=pl.ANY)] + [vmem] * 8,
        out_specs=(vmem, vmem),
        scratch_shapes=[
            pltpu.VMEM((9 * chans, chans), jnp.bfloat16),
            pltpu.VMEM((chans, chans), jnp.bfloat16),
            pltpu.VMEM((chans, chans), jnp.bfloat16),
            pltpu.VMEM((tall, chans), jnp.float32),
            pltpu.VMEM((tall, 3 * chans), jnp.bfloat16),
            pltpu.VMEM((feats, tall), jnp.float32),
            pltpu.SemaphoreType.DMA((3, parts)),
        ],
        compiler_params=pltpu.CompilerParams(vmem_limit_bytes=48 * 2**20),
        cost_estimate=pl.CostEstimate(
            flops=2 * token_rows * chans * chans * 12,
            bytes_accessed=12 * chans * chans * 2,
            transcendentals=4 * token_rows * chans,
        ),
    )(flags, factors, packed, x, noise, key_blocks, value_blocks, bias, gains, w_in, w_final)


def advantages(onehot, own, rewards, own_reward):
    counts = jnp.sum(onehot, axis=0)
    sums = jnp.sum(onehot * rewards[:, None], axis=0)
    squares = jnp.sum(onehot * (rewards * rewards)[:, None], axis=0)
    safe_count = jnp.maximum(counts, 1.0)
    means = sums / safe_count
    spreads = jnp.sqrt(jnp.maximum(squares / safe_count - means * means, 1.0))
    own_mean = jnp.sum(own * means)
    own_spread = jnp.sum(own * spreads)
    return (own_reward - own_mean) / own_spread


def per_device(
    latents,
    noise,
    rewards,
    prompt_ids,
    context,
    time_bias,
    gain_first,
    gain_second,
    gain_third,
    w_in,
    w_conv,
    w_query,
    w_key,
    w_value,
    w_attn_out,
    w_final,
    moment_first,
    moment_second,
):
    sec_count = lax.axis_size("sec")
    dev_count = lax.axis_size("dev")
    prompt_count, context_tokens, _ = context.shape
    assert latents.shape[0] == 1
    col_piece = w_conv.shape[1]
    chans = col_piece * dev_count
    feats = w_in.shape[0] * sec_count
    rows, cols = latents.shape[2] // 2, latents.shape[3] // 2

    pieces = [
        w_conv,
        w_query,
        w_attn_out,
        w_in,
        w_final.astype(jnp.bfloat16).reshape(-1, col_piece),
    ]
    counts = [piece.shape[0] for piece in pieces]
    used = sum(counts)
    unit = 16 * dev_count
    padded = -(-used // unit) * unit
    pieces.append(jnp.zeros((padded - used, col_piece), jnp.bfloat16))
    block = jnp.concatenate(pieces, axis=0)
    block = lax.all_to_all(block, "dev", split_axis=0, concat_axis=1, tiled=True)
    packed = lax.all_gather(block, ("sec", "dev"), axis=0, tiled=True)
    packed = packed.reshape(sec_count, padded, chans)
    at = counts[0] + counts[1] + counts[2]
    in_full = packed[:, at : at + counts[3]].reshape(feats, chans)
    at += counts[3]
    final_full = (
        packed[:, at : at + counts[4]]
        .reshape(sec_count, counts[4], dev_count, col_piece)
        .transpose(0, 2, 1, 3)
        .reshape(sec_count, dev_count, chans // sec_count, feats // dev_count)
        .transpose(0, 2, 1, 3)
        .reshape(chans, feats)
    )
    big = counts[:3]
    if any(count % 16 for count in big):
        packed = jnp.concatenate(
            [
                packed[:, sum(big[:k]) : sum(big[: k + 1])].reshape(-1, chans)
                for k in range(3)
            ],
            axis=0,
        )[None]
        big = [count * sec_count for count in big]

    both = jnp.stack([rewards, prompt_ids.astype(jnp.float32)], axis=1)
    both = doubled_gather(both, "sec")
    all_rewards = both[:, 0]
    catalog = jnp.arange(prompt_count, dtype=jnp.int32)
    onehot = (both[:, 1].astype(jnp.int32)[:, None] == catalog[None, :]).astype(jnp.float32)
    own = (prompt_ids == catalog).astype(jnp.float32)
    advantage = advantages(onehot, own, all_rewards, rewards[0])

    key_rows = w_key.shape[0]
    tokens_up = -(-context_tokens // 16) * 16
    own_context = lax.dynamic_slice_in_dim(
        context, lax.axis_index("sec") * key_rows, key_rows, axis=2
    )
    own_context = jnp.pad(own_context, ((0, 0), (0, tokens_up - context_tokens), (0, 0)))
    partial = jnp.dot(
        own_context.reshape(prompt_count * tokens_up, key_rows),
        jnp.concatenate([w_key, w_value], axis=1),
        preferred_element_type=jnp.float32,
    ).reshape(prompt_count, tokens_up, 2 * col_piece)
    wanted = jnp.einsum(
        "ip,ptc->itc", onehot, partial, precision=lax.Precision.HIGHEST
    )
    own_part = halved_sum(wanted, "sec", jnp.bfloat16).astype(jnp.bfloat16)
    whole = doubled_gather(own_part, "dev").reshape(dev_count, tokens_up, 2, col_piece)
    whole = whole.transpose(2, 1, 0, 3).reshape(2, tokens_up, chans)
    lane = 2 * HEAD
    pairs = chans // lane
    valid = jnp.arange(tokens_up)[None, :, None] < context_tokens
    by_pair = jnp.where(valid, whole, 0).reshape(2, tokens_up, pairs, 2, HEAD)
    by_pair = jnp.pad(by_pair, ((0, 0), (0, lane - tokens_up), (0, 0), (0, 0), (0, 0)))
    eye = jnp.eye(2, dtype=jnp.bfloat16)
    key_blocks = (
        (by_pair[0] * (1.0 / math.sqrt(HEAD))).astype(jnp.bfloat16).transpose(1, 2, 3, 0)[
            :, :, :, None, :
        ]
        * eye[None, :, None, :, None]
    ).reshape(pairs, lane, 2 * lane)
    value_blocks = (
        by_pair[1].transpose(1, 2, 0, 3)[:, :, :, None, :] * eye[None, :, None, :, None]
    ).reshape(pairs, 2 * lane, lane)
    inside = (jnp.arange(lane) < context_tokens).astype(jnp.bfloat16)
    ones = jnp.broadcast_to(
        inside[None, :, None, None] * eye[:, None, :, None], (2, lane, 2, HEAD)
    ).reshape(1, 2 * lane, lane)
    value_blocks = jnp.concatenate(
        [value_blocks, jnp.broadcast_to(ones, value_blocks.shape)], axis=2
    )

    position = lax.axis_index("dev")
    flags = jnp.stack([position > 0, position < dev_count - 1]).astype(jnp.float32)
    planes = jnp.concatenate([latents, noise[:, 0]], axis=0)
    planes = to_tokens(with_halo(planes, "dev", 2, 2 * HALO))
    x, noise_wide = planes[0], planes[1:]
    plans = [plan(k) for k in range(STEPS)]
    factors = jnp.array([(s, b, g, b / g) for s, b, g in plans], jnp.float32)

    gains = jnp.stack([gain_first, gain_second, gain_third])
    rest = (key_blocks, value_blocks, gains, in_full, final_full)
    gradient = jnp.zeros((feats, chans), jnp.float32)
    for first in range(0, STEPS, GROUP):
        if first:
            x = with_halo(x, "dev", 1, HALO * cols)
        part = slice(first, first + GROUP)
        x, share = run_steps(
            rows,
            cols,
            big,
            flags,
            factors[part],
            packed,
            x,
            noise_wide[part],
            rest,
            time_bias[part],
        )
        gradient = gradient + share
    latent = from_tokens(x, rows, cols)[None]

    gradient = gradient * advantage
    row_piece = chans // sec_count
    arranged = gradient.reshape(dev_count, feats // dev_count, sec_count, row_piece)
    arranged = arranged.transpose(2, 0, 1, 3)
    grad_shard = halved_sum(halved_sum(arranged, "sec")[0], "dev")[0].T
    grad_shard = -grad_shard / sec_count
    moment_one = 0.9 * moment_first + 0.1 * grad_shard
    moment_two = 0.999 * moment_second + 0.001 * grad_shard * grad_shard
    new_weight = w_final - learn_rate * moment_one / (jnp.sqrt(moment_two) + 1e-08)
    return (latent, new_weight, moment_one, moment_two)


def solution(mesh):
    weight = P("sec", "dev")
    placed = (
        (P("sec", None, "dev", None), P(None, "sec", None, "dev", None), P("sec"), P("sec"))
        + (P(),) * 5
        + (weight,) * 9
    )
    return jax.shard_map(
        per_device,
        mesh=mesh,
        in_specs=placed,
        out_specs=(P("sec", None, "dev", None), weight, weight, weight),
        check_vma=False,
    )
```

```python
import functools
import math

import jax
import jax.numpy as jnp
from jax import lax
from jax.experimental import pallas as pl
from jax.experimental.pallas import tpu as pltpu
from jax.sharding import PartitionSpec as P

HEAD = 64
STEPS = 6
GROUP = 3
HALO = 4
CHUNK_ROWS = 4

alpha_bars = (0.1, 0.15, 0.21, 0.28, 0.36, 0.45, 0.55)
norm_eps = 1e-06
learn_rate = 0.001


def plan(step_index):
    current = alpha_bars[step_index]
    following = alpha_bars[step_index + 1]
    sigma = math.sqrt((1.0 - following) / (1.0 - current)) * math.sqrt(1.0 - current / following)
    scale = math.sqrt(following / current)
    beta = math.sqrt(1.0 - following - sigma * sigma) - scale * math.sqrt(1.0 - current)
    return (scale, beta, sigma)


def swap(value, axis, mask):
    size = lax.axis_size(axis)
    return lax.ppermute(value, axis, [(i, i ^ mask) for i in range(size)])


def bit_of(axis, mask):
    return (lax.axis_index(axis) & mask) != 0


def doubled_gather(value, axis):
    mask = 1
    while mask < lax.axis_size(axis):
        other = swap(value, axis, mask)
        upper = bit_of(axis, mask)
        value = jnp.concatenate(
            [jnp.where(upper, other, value), jnp.where(upper, value, other)], axis=0
        )
        mask *= 2
    return value


def halved_sum(value, axis, link=jnp.float32):
    mask = lax.axis_size(axis) // 2
    while mask >= 1:
        half = value.shape[0] // 2
        upper = bit_of(axis, mask)
        kept = jnp.where(upper, value[half:], value[:half])
        sent = jnp.where(upper, value[:half], value[half:])
        value = kept + swap(sent.astype(link), axis, mask).astype(value.dtype)
        mask //= 2
    return value


def with_halo(shard, axis, dim, width):
    size, length = (lax.axis_size(axis), shard.shape[dim])
    up = [(i, i + 1) for i in range(size - 1)]
    down = [(j, i) for i, j in up]
    last = lax.slice_in_dim(shard, length - width, length, axis=dim)
    first = lax.slice_in_dim(shard, 0, width, axis=dim)
    before = lax.ppermute(last, axis, up)
    after = lax.ppermute(first, axis, down)
    return jnp.concatenate([before, shard, after], axis=dim)


def lane_order(breadth):
    half = breadth // 2
    lane = jnp.arange(breadth)
    return (lane[:, None] == (2 * (lane % half) + lane // half)[None, :]).astype(jnp.float32)


def to_tokens(latent):
    count, chans, height, breadth = latent.shape
    split = jnp.dot(latent, lane_order(breadth), precision=lax.Precision.HIGHEST)
    blocks = split.reshape(count, chans, height // 2, 2, 2, breadth // 2)
    return blocks.transpose(0, 1, 3, 4, 2, 5).reshape(
        count, chans * 4, height * breadth // 4
    )


def from_tokens(tokens, rows, cols):
    feats = tokens.shape[0]
    blocks = tokens.reshape(feats // 4, 2, 2, rows, cols).transpose(0, 3, 1, 2, 4)
    return jnp.dot(
        blocks.reshape(feats // 4, 2 * rows, 2 * cols),
        lane_order(2 * cols).T,
        precision=lax.Precision.HIGHEST,
    )


def rms_scale(values, gain):
    mean_square = jnp.mean(values * values, axis=-1, keepdims=True)
    return values * lax.rsqrt(mean_square + norm_eps) * gain


def silu(values):
    return 0.5 * values * (1.0 + jnp.tanh(0.5 * values))


def weight_copies(core, counts, sources, targets, sems):
    if len(sources) == 1:
        blocks = [(sources[0].at[part], 0, part) for part in range(sources[0].shape[0])]
        length = sources[0].shape[1]
    else:
        parts, halves, length, _ = sources[0].shape
        blocks = [
            (sources[0 if c == core else 1].at[part, half], (2 * half + c) * length, part)
            for part in range(parts)
            for half in range(halves)
            for c in range(2)
        ]
    copies = ([], [], [])
    for block, first, part in blocks:
        offset = 0
        for which, (count, target) in enumerate(zip(counts, targets)):
            low, high = max(first, offset), min(first + length, offset + count)
            if low < high:
                copies[which].append(
                    pltpu.make_async_copy(
                        block.at[pl.ds(low - first, high - low)],
                        target.at[pl.ds(part * count + low - offset, high - low)],
                        sems.at[which, len(copies[which])],
                    )
                )
            offset += count
    return copies


def steps_kernel(
    rows,
    cols,
    counts,
    source_count,
    flags,
    factors,
    *refs,
):
    sources = refs[:source_count]
    (
        x_in,
        noise,
        key_blocks,
        value_blocks,
        bias,
        gains,
        w_in,
        w_final,
        x_out,
        grad_out,
        w_conv,
        w_plus,
        w_query,
        w_attn,
        hidden,
        columns,
        state,
        sems,
    ) = refs[source_count:]
    group = bias.shape[0]
    feats, chans = w_in.shape
    targets = (w_conv, w_query, w_attn)

    def each_core(act):
        if source_count == 1:
            act(weight_copies(0, counts, sources, targets, sems))
            return
        for core in range(2):

            @pl.when(flags[2] == core)
            def _():
                act(weight_copies(core, counts, sources, targets, sems))

    def start_all(copies):
        for some in copies:
            for copy in some:
                copy.start()

    def wait_all(copies):
        for some in copies:
            for copy in some:
                copy.wait()

    each_core(start_all)
    state[...] = x_in[...]
    grad_out[...] = jnp.zeros_like(grad_out)
    columns[...] = jnp.zeros_like(columns)
    pairs = key_blocks.shape[0]
    wide = 2 * HEAD
    size = CHUNK_ROWS * cols
    token = lax.broadcasted_iota(jnp.int32, (size, 1), 0)
    lane_token = lax.broadcasted_iota(jnp.int32, (1, size), 1)
    col = lax.rem(token, cols)
    taps = 3 * chans

    def activate(step, chunk):
        start = pl.multiple_of(chunk * size, size)
        before_norm = (
            lax.dot_general(
                state[:, pl.ds(start, size)].astype(jnp.bfloat16),
                w_in[...],
                (((0,), (0,)), ((), ())),
                preferred_element_type=jnp.float32,
            )
            + bias[pl.ds(step, 1), :]
        )
        first = chunk * (CHUNK_ROWS // 2)
        hidden[pl.ds(first, CHUNK_ROWS // 2)] = before_norm.reshape(
            CHUNK_ROWS // 2, 2, cols, chans
        )
        act = silu(rms_scale(before_norm, gains[0:1, :]))
        inside = jnp.where(
            start + token < HALO * cols,
            flags[0],
            jnp.where(start + token >= (HALO + rows) * cols, flags[1], 1),
        )
        act = act * inside.astype(jnp.float32)
        left = jnp.where(col == 0, 0.0, pltpu.roll(act, 1, 0))
        right = jnp.where(col == cols - 1, 0.0, pltpu.roll(act, size - 1, 0))
        for which, value in enumerate((left, act, right)):
            value = value.astype(jnp.bfloat16)
            for row in range(CHUNK_ROWS):
                columns[
                    first + (row + 1) // 2, (row + 1) % 2, :, which * chans : (which + 1) * chans
                ] = value[row * cols : (row + 1) * cols]

    twos = (rows + HALO) // 4

    def convolve(part, carry):
        at = 1 + part * twos
        above, upper = columns[pl.ds(at, twos), 0], columns[pl.ds(at, twos), 1]
        lower, below = columns[pl.ds(at + 1, twos), 0], columns[pl.ds(at + 1, twos), 1]

        def product(value, weight):
            return jnp.dot(
                value.reshape(twos * cols, taps), weight, preferred_element_type=jnp.float32
            )

        plus = product(upper + lower, w_plus[...])
        minus = product(lower - upper, w_conv[taps : 2 * taps, :])
        span = pl.ds(at, twos)
        even = plus + minus + product(above - lower, w_conv[:taps, :])
        hidden[span, 0] += even.reshape(twos, cols, chans)
        odd = plus - minus - product(upper - below, w_conv[2 * taps :, :])
        hidden[span, 1] += odd.reshape(twos, cols, chans)
        return carry

    def finish(step, start):
        row_pair = lax.div(start, 2 * cols)
        mixed = hidden[pl.ds(row_pair, CHUNK_ROWS // 2)].reshape(size, chans)
        normed = rms_scale(mixed, gains[1:2, :]).astype(jnp.bfloat16)
        queries = jnp.dot(normed, w_query[...], preferred_element_type=jnp.float32).astype(
            jnp.bfloat16
        )
        heads = []
        for pair in range(pairs):
            scores = jnp.dot(
                queries[:, pair * wide : (pair + 1) * wide],
                key_blocks[pair],
                preferred_element_type=jnp.float32,
            )
            sums = jnp.dot(
                jnp.exp(scores).astype(jnp.bfloat16),
                value_blocks[pair],
                preferred_element_type=jnp.float32,
            )
            heads.append((sums[:, :wide] / sums[:, wide:]).astype(jnp.bfloat16))
        attended = jnp.concatenate(heads, axis=1)
        output = mixed + jnp.dot(attended, w_attn[...], preferred_element_type=jnp.float32)
        act = silu(rms_scale(output, gains[2:3, :])).astype(jnp.bfloat16)
        predicted = jnp.dot(act, w_final[...], preferred_element_type=jnp.float32)
        span = pl.ds(start, size)
        noise_now = noise[step, :, span]
        state[:, span] = (
            factors[step, 0] * state[:, span]
            + factors[step, 1] * predicted.T
            + factors[step, 2] * noise_now
        )
        place = start + lane_token
        own = (place >= HALO * cols) & (place < (HALO + rows) * cols)
        weights = jnp.where(own, noise_now, 0.0)
        upper = weights.astype(jnp.bfloat16)
        lower = (weights - upper.astype(jnp.float32)).astype(jnp.bfloat16)
        share = jnp.dot(
            jnp.concatenate([upper, lower], axis=0), act, preferred_element_type=jnp.float32
        )
        grad_out[...] += factors[step, 3] * (share[:feats] + share[feats:])

    chunks = state.shape[1] // size

    def one_step(step, carry):
        def fill(chunk, carry):
            activate(step, chunk)
            return carry

        lax.fori_loop(0, chunks, fill, 0)

        @pl.when(step == 0)
        def _():
            each_core(wait_all)
            block = chans // 5

            def combine(number, carry):
                here = pl.multiple_of(number * block, block)
                first, middle, final = (
                    w_conv[pl.ds(tap * taps + here, block), :].astype(jnp.float32)
                    for tap in range(3)
                )
                outer = 0.5 * (first + final)
                w_plus[pl.ds(here, block), :] = (outer + 0.5 * middle).astype(jnp.bfloat16)
                w_conv[pl.ds(taps + here, block), :] = (outer - 0.5 * middle).astype(
                    jnp.bfloat16
                )
                return carry

            lax.fori_loop(0, taps // block, combine, 0)

        lax.fori_loop(0, 2, convolve, 0)
        last = step == group - 1
        base = jnp.where(last, HALO, HALO // 2) * cols

        def rest(number, carry):
            finish(step, pl.multiple_of(base + number * size, 2 * cols))
            return carry

        lax.fori_loop(0, jnp.where(last, chunks - 2, chunks - 1), rest, 0)
        return carry

    lax.fori_loop(0, group, one_step, 0)
    x_out[...] = state[:, HALO * cols : (HALO + rows) * cols]


def run_steps(rows, cols, counts, flags, factors, sources, x, noise, rest, bias):
    key_blocks, value_blocks, gains, w_in, w_final = rest
    feats, chans = w_in.shape
    tall_rows = rows + 2 * HALO
    vmem = pl.BlockSpec(memory_space=pltpu.VMEM)
    smem = pl.BlockSpec(memory_space=pltpu.SMEM)
    token_rows = sum(rows + 2 * k for k in range(GROUP)) * cols
    most = sources[0].shape[0] * (1 if len(sources) == 1 else 2 * sources[0].shape[1])
    return pl.pallas_call(
        functools.partial(steps_kernel, rows, cols, counts, len(sources)),
        out_shape=(
            jax.ShapeDtypeStruct((feats, rows * cols), jnp.float32),
            jax.ShapeDtypeStruct((feats, chans), jnp.float32),
        ),
        in_specs=[smem, smem]
        + [pl.BlockSpec(memory_space=pl.ANY)] * len(sources)
        + [vmem] * 8,
        out_specs=(vmem, vmem),
        scratch_shapes=[
            pltpu.VMEM((9 * chans, chans), jnp.bfloat16),
            pltpu.VMEM((3 * chans, chans), jnp.bfloat16),
            pltpu.VMEM((chans, chans), jnp.bfloat16),
            pltpu.VMEM((chans, chans), jnp.bfloat16),
            pltpu.VMEM((tall_rows // 2, 2, cols, chans), jnp.float32),
            pltpu.VMEM((tall_rows // 2 + 1, 2, cols, 3 * chans), jnp.bfloat16),
            pltpu.VMEM((feats, tall_rows * cols), jnp.float32),
            pltpu.SemaphoreType.DMA((3, most)),
        ],
        compiler_params=pltpu.CompilerParams(vmem_limit_bytes=52 * 2**20),
        cost_estimate=pl.CostEstimate(
            flops=2 * token_rows * chans * chans * 12,
            bytes_accessed=12 * chans * chans * 2,
            transcendentals=4 * token_rows * chans,
        ),
    )(flags, factors, *sources, x, noise, key_blocks, value_blocks, bias, gains, w_in, w_final)


def advantages(onehot, own, rewards, own_reward):
    counts = jnp.sum(onehot, axis=0)
    sums = jnp.sum(onehot * rewards[:, None], axis=0)
    squares = jnp.sum(onehot * (rewards * rewards)[:, None], axis=0)
    safe_count = jnp.maximum(counts, 1.0)
    means = sums / safe_count
    spreads = jnp.sqrt(jnp.maximum(squares / safe_count - means * means, 1.0))
    own_mean = jnp.sum(own * means)
    own_spread = jnp.sum(own * spreads)
    return (own_reward - own_mean) / own_spread


def per_device(
    latents,
    noise,
    rewards,
    prompt_ids,
    context,
    time_bias,
    gain_first,
    gain_second,
    gain_third,
    w_in,
    w_conv,
    w_query,
    w_key,
    w_value,
    w_attn_out,
    w_final,
    moment_first,
    moment_second,
):
    sec_count = lax.axis_size("sec")
    dev_count = lax.axis_size("dev")
    prompt_count, context_tokens, _ = context.shape
    assert latents.shape[0] == 1
    col_piece = w_conv.shape[1]
    chans = col_piece * dev_count
    feats = w_in.shape[0] * sec_count
    rows, cols = latents.shape[2] // 2, latents.shape[3] // 2

    pieces = [
        w_conv,
        w_query,
        w_attn_out,
        w_in,
        w_final.astype(jnp.bfloat16).reshape(-1, col_piece),
    ]
    counts = [piece.shape[0] for piece in pieces]
    used = sum(counts)
    unit = 16 * dev_count
    padded = -(-used // unit) * unit
    pieces.append(jnp.zeros((padded - used, col_piece), jnp.bfloat16))
    block = jnp.concatenate(pieces, axis=0)
    block = lax.all_to_all(block, "dev", split_axis=0, concat_axis=1, tiled=True)
    total = sec_count * dev_count
    mates = [list(range(core, total, 2)) for core in range(2)]
    mine = lax.all_gather(block, ("sec", "dev"), axis=0, tiled=True, axis_index_groups=mates)
    theirs = swap(mine, "dev", 1)
    core = lax.axis_index("dev") % 2
    length = padded // dev_count
    mine = mine.reshape(sec_count, dev_count // 2, length, chans)
    theirs = theirs.reshape(mine.shape)

    def rows_of(first, count, local):
        if local and first // length == (first + count - 1) // length:
            half, which = divmod(first // length, 2)
            inner = slice(first % length, first % length + count)
            return jnp.where(core == which, mine[:, half, inner], theirs[:, half, inner])
        everything = jnp.where(
            core == 0, jnp.stack([mine, theirs], axis=2), jnp.stack([theirs, mine], axis=2)
        )
        return everything.reshape(sec_count, padded, chans)[:, first : first + count]

    at = counts[0] + counts[1] + counts[2]
    small = rows_of(at, counts[3] + counts[4], True)
    in_full = small[:, : counts[3]].reshape(feats, chans)
    final_full = (
        small[:, counts[3] :]
        .reshape(sec_count, counts[4], dev_count, col_piece)
        .transpose(0, 2, 1, 3)
        .reshape(sec_count, dev_count, chans // sec_count, feats // dev_count)
        .transpose(0, 2, 1, 3)
        .reshape(chans, feats)
    )
    big = counts[:3]
    sources = (mine, theirs)
    if any(count % 16 for count in big):
        first = [sum(big[:k]) for k in range(3)]
        sources = (
            jnp.concatenate(
                [rows_of(f, c, False).reshape(-1, chans) for f, c in zip(first, big)], axis=0
            )[None],
        )
        big = [count * sec_count for count in big]

    both = jnp.stack([rewards, prompt_ids.astype(jnp.float32)], axis=1)
    both = doubled_gather(both, "sec")
    all_rewards = both[:, 0]
    catalog = jnp.arange(prompt_count, dtype=jnp.int32)
    onehot = (both[:, 1].astype(jnp.int32)[:, None] == catalog[None, :]).astype(jnp.float32)
    own = (prompt_ids == catalog).astype(jnp.float32)
    advantage = advantages(onehot, own, all_rewards, rewards[0])

    key_rows = w_key.shape[0]
    tokens_up = -(-context_tokens // 16) * 16
    own_context = lax.dynamic_slice_in_dim(
        context, lax.axis_index("sec") * key_rows, key_rows, axis=2
    )
    own_context = jnp.pad(own_context, ((0, 0), (0, tokens_up - context_tokens), (0, 0)))
    partial = jnp.dot(
        own_context.reshape(prompt_count * tokens_up, key_rows),
        jnp.concatenate([w_key, w_value], axis=1),
        preferred_element_type=jnp.float32,
    ).reshape(prompt_count, tokens_up, 2 * col_piece)
    wanted = jnp.einsum(
        "ip,ptc->itc", onehot, partial, precision=lax.Precision.HIGHEST
    )
    own_part = halved_sum(wanted, "sec", jnp.bfloat16).astype(jnp.bfloat16)
    whole = doubled_gather(own_part, "dev").reshape(dev_count, tokens_up, 2, col_piece)
    whole = whole.transpose(2, 1, 0, 3).reshape(2, tokens_up, chans)
    lane = 2 * HEAD
    pairs = chans // lane
    valid = jnp.arange(tokens_up)[None, :, None] < context_tokens
    by_pair = jnp.where(valid, whole, 0).reshape(2, tokens_up, pairs, 2, HEAD)
    by_pair = jnp.pad(by_pair, ((0, 0), (0, lane - tokens_up), (0, 0), (0, 0), (0, 0)))
    eye = jnp.eye(2, dtype=jnp.bfloat16)
    key_blocks = (
        (by_pair[0] * (1.0 / math.sqrt(HEAD))).astype(jnp.bfloat16).transpose(1, 2, 3, 0)[
            :, :, :, None, :
        ]
        * eye[None, :, None, :, None]
    ).reshape(pairs, lane, 2 * lane)
    value_blocks = (
        by_pair[1].transpose(1, 2, 0, 3)[:, :, :, None, :] * eye[None, :, None, :, None]
    ).reshape(pairs, 2 * lane, lane)
    inside = (jnp.arange(lane) < context_tokens).astype(jnp.bfloat16)
    ones = jnp.broadcast_to(
        inside[None, :, None, None] * eye[:, None, :, None], (2, lane, 2, HEAD)
    ).reshape(1, 2 * lane, lane)
    value_blocks = jnp.concatenate(
        [value_blocks, jnp.broadcast_to(ones, value_blocks.shape)], axis=2
    )

    position = lax.axis_index("dev")
    flags = jnp.stack([position > 0, position < dev_count - 1, core == 1]).astype(jnp.int32)
    planes = jnp.concatenate([latents, noise[:, 0]], axis=0)
    planes = to_tokens(with_halo(planes, "dev", 2, 2 * HALO))
    x, noise_wide = planes[0], planes[1:]
    plans = [plan(k) for k in range(STEPS)]
    factors = jnp.array([(s, b, g, b / g) for s, b, g in plans], jnp.float32)

    gains = jnp.stack([gain_first, gain_second, gain_third])
    rest = (key_blocks, value_blocks, gains, in_full, final_full)
    gradient = jnp.zeros((feats, chans), jnp.float32)
    for first in range(0, STEPS, GROUP):
        if first:
            x = with_halo(x, "dev", 1, HALO * cols)
        part = slice(first, first + GROUP)
        x, share = run_steps(
            rows,
            cols,
            big,
            flags,
            factors[part],
            sources,
            x,
            noise_wide[part],
            rest,
            time_bias[part],
        )
        gradient = gradient + share
    latent = from_tokens(x, rows, cols)[None]

    gradient = gradient * advantage
    row_piece = chans // sec_count
    arranged = gradient.reshape(dev_count, feats // dev_count, sec_count, row_piece)
    arranged = arranged.transpose(2, 0, 1, 3).reshape(total, -1)
    arrived = lax.all_to_all(arranged, ("sec", "dev"), split_axis=0, concat_axis=0, tiled=True)
    grad_shard = jnp.sum(arrived, axis=0).reshape(feats // dev_count, row_piece).T
    grad_shard = -grad_shard / sec_count
    moment_one = 0.9 * moment_first + 0.1 * grad_shard
    moment_two = 0.999 * moment_second + 0.001 * grad_shard * grad_shard
    new_weight = w_final - learn_rate * moment_one / (jnp.sqrt(moment_two) + 1e-08)
    return (latent, new_weight, moment_one, moment_two)


def solution(mesh):
    weight = P("sec", "dev")
    placed = (
        (P("sec", None, "dev", None), P(None, "sec", None, "dev", None), P("sec"), P("sec"))
        + (P(),) * 5
        + (weight,) * 9
    )
    return jax.shard_map(
        per_device,
        mesh=mesh,
        in_specs=placed,
        out_specs=(P("sec", None, "dev", None), weight, weight, weight),
        check_vma=False,
    )
```

```python
import functools
import math

import jax
import jax.numpy as jnp
from jax import lax
from jax.experimental import pallas as pl
from jax.experimental.pallas import tpu as pltpu
from jax.sharding import PartitionSpec as P

HEAD = 64
STEPS = 6
GROUP = 3
HALO = 4
CHUNK_ROWS = 4

alpha_bars = (0.1, 0.15, 0.21, 0.28, 0.36, 0.45, 0.55)
norm_eps = 1e-06
learn_rate = 0.001


def plan(step_index):
    current = alpha_bars[step_index]
    following = alpha_bars[step_index + 1]
    sigma = math.sqrt((1.0 - following) / (1.0 - current)) * math.sqrt(1.0 - current / following)
    scale = math.sqrt(following / current)
    beta = math.sqrt(1.0 - following - sigma * sigma) - scale * math.sqrt(1.0 - current)
    return (scale, beta, sigma)


def swap(value, axis, mask):
    size = lax.axis_size(axis)
    return lax.ppermute(value, axis, [(i, i ^ mask) for i in range(size)])


def bit_of(axis, mask):
    return (lax.axis_index(axis) & mask) != 0


def doubled_gather(value, axis):
    mask = 1
    while mask < lax.axis_size(axis):
        other = swap(value, axis, mask)
        upper = bit_of(axis, mask)
        value = jnp.concatenate(
            [jnp.where(upper, other, value), jnp.where(upper, value, other)], axis=0
        )
        mask *= 2
    return value


def halved_sum(value, axis, link=jnp.float32):
    mask = lax.axis_size(axis) // 2
    while mask >= 1:
        half = value.shape[0] // 2
        upper = bit_of(axis, mask)
        kept = jnp.where(upper, value[half:], value[:half])
        sent = jnp.where(upper, value[:half], value[half:])
        value = kept + swap(sent.astype(link), axis, mask).astype(value.dtype)
        mask //= 2
    return value


def with_halo(shard, axis, dim, width):
    size, length = (lax.axis_size(axis), shard.shape[dim])
    up = [(i, i + 1) for i in range(size - 1)]
    down = [(j, i) for i, j in up]
    last = lax.slice_in_dim(shard, length - width, length, axis=dim)
    first = lax.slice_in_dim(shard, 0, width, axis=dim)
    before = lax.ppermute(last, axis, up)
    after = lax.ppermute(first, axis, down)
    return jnp.concatenate([before, shard, after], axis=dim)


def lane_order(breadth):
    half = breadth // 2
    lane = jnp.arange(breadth)
    return (lane[:, None] == (2 * (lane % half) + lane // half)[None, :]).astype(jnp.float32)


def to_tokens(latent):
    count, chans, height, breadth = latent.shape
    split = jnp.dot(latent, lane_order(breadth), precision=lax.Precision.HIGHEST)
    blocks = split.reshape(count, chans, height // 2, 2, 2, breadth // 2)
    return blocks.transpose(0, 1, 3, 4, 2, 5).reshape(
        count, chans * 4, height * breadth // 4
    )


def from_tokens(tokens, rows, cols):
    feats = tokens.shape[0]
    blocks = tokens.reshape(feats // 4, 2, 2, rows, cols).transpose(0, 3, 1, 2, 4)
    return jnp.dot(
        blocks.reshape(feats // 4, 2 * rows, 2 * cols),
        lane_order(2 * cols).T,
        precision=lax.Precision.HIGHEST,
    )


def rms_scale(values, gain):
    mean_square = jnp.mean(values * values, axis=-1, keepdims=True)
    return values * lax.rsqrt(mean_square + norm_eps) * gain


def silu_of_twice(values):
    return values + values * jnp.tanh(values)


def weight_copies(counts, split, relative, flags, refs, targets, sems):
    main, pieces = refs[0], refs[1:]
    copies = ([], [], [])

    def add(which, source, target):
        number = len(copies[which])
        copies[which].append(pltpu.make_async_copy(source, target, sems.at[which, number]))

    for part in range(main.shape[0]):
        offset = 0
        for which, (count, target) in enumerate(zip(counts, targets)):
            here = split if which == 0 else count
            add(
                which,
                main.at[part, pl.ds(offset, here)],
                target.at[pl.ds(part * count, here)],
            )
            offset += here
    for piece, places in zip(pieces, relative):
        for number, (sec, dev) in enumerate(places):
            length = piece.shape[1]
            row = (flags[2] ^ sec) * counts[0] + split + (flags[3] ^ dev) * length
            row = pl.multiple_of(row, 16)
            add(0, piece.at[number], targets[0].at[pl.ds(row, length)])
    return copies


def interleave(*tasks):
    tasks = list(tasks)
    while tasks:
        for task in list(tasks):
            try:
                next(task)
            except StopIteration:
                tasks.remove(task)


def steps_kernel(
    rows,
    cols,
    counts,
    split,
    relative,
    flags,
    factors,
    *refs,
):
    source_count = 1 + len(relative)
    sources = refs[:source_count]
    (
        x_in,
        noise,
        key_blocks,
        value_blocks,
        bias,
        gains,
        w_in,
        w_final,
        x_out,
        grad_out,
        w_conv,
        w_plus,
        w_query,
        w_attn,
        hidden,
        columns,
        state,
        sems,
    ) = refs[source_count:]
    group = bias.shape[0]
    feats, chans = w_in.shape
    copies = weight_copies(
        counts, split, relative, flags, sources, (w_conv, w_query, w_attn), sems
    )
    for some in copies:
        for copy in some:
            copy.start()
    state[...] = x_in[...]
    grad_out[...] = jnp.zeros_like(grad_out)
    pairs = key_blocks.shape[0]
    wide = 2 * HEAD
    size = CHUNK_ROWS * cols
    lane_token = lax.broadcasted_iota(jnp.int32, (1, size), 1)
    edge = 16
    near = lax.broadcasted_iota(jnp.int32, (edge, 1), 0)
    taps = 3 * chans

    def activate(step, start):
        before_norm = (
            lax.dot_general(
                state[:, pl.ds(start, size)].astype(jnp.bfloat16),
                w_in[...],
                (((0,), (0,)), ((), ())),
                preferred_element_type=jnp.float32,
            )
            + bias[pl.ds(step, 1), :]
        )
        first = lax.div(start, 2 * cols)
        yield
        for row in range(CHUNK_ROWS):
            value = before_norm[row * cols : (row + 1) * cols]
            hidden[first + row // 2, row % 2] = value
            act = silu_of_twice(rms_scale(value, gains[0:1, :]))
            place = 2 * first + row
            inside = jnp.where(
                place < HALO, flags[0], jnp.where(place >= HALO + rows, flags[1], 1)
            )
            act = act * inside.astype(jnp.float32)
            at = (first + (row + 1) // 2, (row + 1) % 2)
            left = pltpu.roll(act, 1, 0)
            right = pltpu.roll(act, cols - 1, 0)
            first_left = jnp.where(near == 0, 0.0, left[:edge])
            last_right = jnp.where(near == edge - 1, 0.0, right[cols - edge :])
            columns[at + (slice(0, edge), slice(0, chans))] = first_left.astype(jnp.bfloat16)
            columns[at + (slice(edge, cols), slice(0, chans))] = left[edge:].astype(jnp.bfloat16)
            columns[at + (slice(0, cols), slice(chans, 2 * chans))] = act.astype(jnp.bfloat16)
            columns[at + (slice(0, cols - edge), slice(2 * chans, taps))] = right[
                : cols - edge
            ].astype(jnp.bfloat16)
            columns[at + (slice(cols - edge, cols), slice(2 * chans, taps))] = last_right.astype(
                jnp.bfloat16
            )
            yield

    twos = (rows + HALO) // 4

    def convolve(part, carry):
        at = 1 + part * twos
        above, upper = columns[pl.ds(at, twos), 0], columns[pl.ds(at, twos), 1]
        lower, below = columns[pl.ds(at + 1, twos), 0], columns[pl.ds(at + 1, twos), 1]

        def product(value, weight):
            return jnp.dot(
                value.reshape(twos * cols, taps), weight, preferred_element_type=jnp.float32
            )

        plus = product(upper + lower, w_plus[...])
        minus = product(lower - upper, w_conv[taps : 2 * taps, :])
        span = pl.ds(at, twos)
        even = plus + minus + product(above - lower, w_conv[:taps, :])
        hidden[span, 0] += even.reshape(twos, cols, chans)
        odd = plus - minus - product(upper - below, w_conv[2 * taps :, :])
        hidden[span, 1] += odd.reshape(twos, cols, chans)
        return carry

    def finish(step, start):
        row_pair = lax.div(start, 2 * cols)
        mixed = hidden[pl.ds(row_pair, CHUNK_ROWS // 2)].reshape(size, chans)
        normed = rms_scale(mixed, gains[1:2, :]).astype(jnp.bfloat16)
        yield
        queries = jnp.dot(normed, w_query[...], preferred_element_type=jnp.float32).astype(
            jnp.bfloat16
        )
        yield
        heads = []
        for pair in range(pairs):
            scores = jnp.dot(
                queries[:, pair * wide : (pair + 1) * wide],
                key_blocks[pair],
                preferred_element_type=jnp.float32,
            )
            sums = jnp.dot(
                jnp.exp(scores).astype(jnp.bfloat16),
                value_blocks[pair],
                preferred_element_type=jnp.float32,
            )
            heads.append(
                (sums[:, :wide] * pl.reciprocal(sums[:, wide:], approx=True)).astype(
                    jnp.bfloat16
                )
            )
            yield
        attended = jnp.concatenate(heads, axis=1)
        output = mixed + jnp.dot(attended, w_attn[...], preferred_element_type=jnp.float32)
        act = silu_of_twice(rms_scale(output, gains[2:3, :])).astype(jnp.bfloat16)
        predicted = jnp.dot(act, w_final[...], preferred_element_type=jnp.float32)
        span = pl.ds(start, size)
        noise_now = noise[step, :, span]
        state[:, span] = (
            factors[step, 0] * state[:, span]
            + factors[step, 1] * predicted.T
            + factors[step, 2] * noise_now
        )
        place = start + lane_token
        own = (place >= HALO * cols) & (place < (HALO + rows) * cols)
        weights = jnp.where(own, noise_now, 0.0)
        upper = weights.astype(jnp.bfloat16)
        lower = (weights - upper.astype(jnp.float32)).astype(jnp.bfloat16)
        share = jnp.dot(
            jnp.concatenate([upper, lower], axis=0), act, preferred_element_type=jnp.float32
        )
        grad_out[...] += factors[step, 3] * (share[:feats] + share[feats:])

    chunks = state.shape[1] // size

    def fill(chunk, carry):
        interleave(activate(0, pl.multiple_of(chunk * size, size)))
        return carry

    lax.fori_loop(0, chunks, fill, 0)
    for some in copies:
        for copy in some:
            copy.wait()
    block = chans // 5

    def combine(number, carry):
        here = pl.multiple_of(number * block, block)
        first, middle, final = (
            w_conv[pl.ds(tap * taps + here, block), :].astype(jnp.float32) for tap in range(3)
        )
        outer = 0.5 * (first + final)
        w_plus[pl.ds(here, block), :] = (outer + 0.5 * middle).astype(jnp.bfloat16)
        w_conv[pl.ds(taps + here, block), :] = (outer - 0.5 * middle).astype(jnp.bfloat16)
        return carry

    lax.fori_loop(0, taps // block, combine, 0)

    def one_step(step, carry):
        lax.fori_loop(0, 2, convolve, 0)
        last = step == group - 1
        base = jnp.where(last, HALO, HALO // 2) * cols
        count = jnp.where(last, chunks - 2, chunks - 1)
        after = jnp.minimum(step + 1, group - 1)

        def place(number):
            return pl.multiple_of(base + number * size, 2 * cols)

        def rest(number, carry):
            interleave(
                finish(step, place(number)), activate(after, place(jnp.maximum(number - 1, 0)))
            )
            return carry

        lax.fori_loop(0, count, rest, 0)

        @pl.when(step < group - 1)
        def _():
            interleave(activate(after, place(count - 1)))

        return carry

    lax.fori_loop(0, group, one_step, 0)
    x_out[...] = state[:, HALO * cols : (HALO + rows) * cols]


def run_steps(rows, cols, counts, split, relative, flags, factors, sources, x, noise, rest, bias):
    key_blocks, value_blocks, gains, w_in, w_final = rest
    feats, chans = w_in.shape
    tall_rows = rows + 2 * HALO
    vmem = pl.BlockSpec(memory_space=pltpu.VMEM)
    smem = pl.BlockSpec(memory_space=pltpu.SMEM)
    token_rows = sum(rows + 2 * k for k in range(GROUP)) * cols
    most = sources[0].shape[0] + sum(len(places) for places in relative)
    return pl.pallas_call(
        functools.partial(steps_kernel, rows, cols, counts, split, relative),
        out_shape=(
            jax.ShapeDtypeStruct((feats, rows * cols), jnp.float32),
            jax.ShapeDtypeStruct((feats, chans), jnp.float32),
        ),
        in_specs=[smem, smem]
        + [pl.BlockSpec(memory_space=pl.ANY)] * len(sources)
        + [vmem] * 8,
        out_specs=(vmem, vmem),
        scratch_shapes=[
            pltpu.VMEM((9 * chans, chans), jnp.bfloat16),
            pltpu.VMEM((3 * chans, chans), jnp.bfloat16),
            pltpu.VMEM((chans, chans), jnp.bfloat16),
            pltpu.VMEM((chans, chans), jnp.bfloat16),
            pltpu.VMEM((tall_rows // 2, 2, cols, chans), jnp.float32),
            pltpu.VMEM((tall_rows // 2 + 1, 2, cols, 3 * chans), jnp.bfloat16),
            pltpu.VMEM((feats, tall_rows * cols), jnp.float32),
            pltpu.SemaphoreType.DMA((3, most)),
        ],
        compiler_params=pltpu.CompilerParams(vmem_limit_bytes=52 * 2**20),
        cost_estimate=pl.CostEstimate(
            flops=2 * token_rows * chans * chans * 12,
            bytes_accessed=12 * chans * chans * 2,
            transcendentals=4 * token_rows * chans,
        ),
    )(flags, factors, *sources, x, noise, key_blocks, value_blocks, bias, gains, w_in, w_final)


def advantages(onehot, own, rewards, own_reward):
    counts = jnp.sum(onehot, axis=0)
    sums = jnp.sum(onehot * rewards[:, None], axis=0)
    squares = jnp.sum(onehot * (rewards * rewards)[:, None], axis=0)
    safe_count = jnp.maximum(counts, 1.0)
    means = sums / safe_count
    spreads = jnp.sqrt(jnp.maximum(squares / safe_count - means * means, 1.0))
    own_mean = jnp.sum(own * means)
    own_spread = jnp.sum(own * spreads)
    return (own_reward - own_mean) / own_spread


def per_device(
    latents,
    noise,
    rewards,
    prompt_ids,
    context,
    time_bias,
    gain_first,
    gain_second,
    gain_third,
    w_in,
    w_conv,
    w_query,
    w_key,
    w_value,
    w_attn_out,
    w_final,
    moment_first,
    moment_second,
):
    sec_count = lax.axis_size("sec")
    dev_count = lax.axis_size("dev")
    prompt_count, context_tokens, _ = context.shape
    assert latents.shape[0] == 1
    col_piece = w_conv.shape[1]
    chans = col_piece * dev_count
    feats = w_in.shape[0] * sec_count
    rows, cols = latents.shape[2] // 2, latents.shape[3] // 2

    pieces = [
        w_conv,
        w_query,
        w_attn_out,
        w_in,
        w_final.astype(jnp.bfloat16).reshape(-1, col_piece),
    ]
    counts = [piece.shape[0] for piece in pieces]
    big = counts[:3]
    used = sum(counts)
    unit = 16 * dev_count
    padded = -(-used // unit) * unit
    whole_tiles = all(count % 16 == 0 for count in big)
    doubled = int(padded * 0.36) // unit * unit if whole_tiles else 0
    split = counts[0] - doubled
    pieces = [w_conv[:split]] + pieces[1:]
    pieces.append(jnp.zeros((padded - used, col_piece), jnp.bfloat16))
    blocks = [jnp.concatenate(pieces, axis=0), w_conv[split:]]
    main_length, length = (padded - doubled) // dev_count, doubled // dev_count
    block = jnp.concatenate([b.reshape(dev_count, -1, col_piece) for b in blocks], axis=1)
    block = block.reshape(padded, col_piece)
    block = lax.all_to_all(block, "dev", split_axis=0, concat_axis=1, tiled=True)
    packed = lax.all_gather(block[:main_length], ("sec", "dev"), axis=0, tiled=True)
    packed = packed.reshape(sec_count, padded - doubled, chans)
    sources, relative = [packed], []
    if doubled:
        turns = [("dev", 1 << k) for k in range(1, dev_count.bit_length() - 1)]
        turns += [("sec", 1 << k) for k in range(1, sec_count.bit_length() - 1)]
        turns += [("sec", 1), ("dev", 1)]
        held, places = [block[main_length:][None]], [((0, 0),)]
        for number, (axis, mask) in enumerate(turns):
            step = (mask, 0) if axis == "sec" else (0, mask)
            new = [swap(piece, axis, mask) for piece in held]
            new_places = [tuple((s ^ step[0], d ^ step[1]) for s, d in p) for p in places]
            if number < len(turns) - 2:
                held = [jnp.concatenate(held + new, axis=0)]
                places = [places[0] + new_places[0]]
            else:
                held, places = held + new, places + new_places
        sources, relative = sources + held, places

    at = split + counts[1] + counts[2]
    in_full = packed[:, at : at + counts[3]].reshape(feats, chans)
    at += counts[3]
    final_full = (
        packed[:, at : at + counts[4]]
        .reshape(sec_count, counts[4], dev_count, col_piece)
        .transpose(0, 2, 1, 3)
        .reshape(sec_count, dev_count, chans // sec_count, feats // dev_count)
        .transpose(0, 2, 1, 3)
        .reshape(chans, feats)
    )
    if not whole_tiles:
        first = [sum(big[:k]) for k in range(3)]
        sources = [
            jnp.concatenate(
                [packed[:, f : f + c].reshape(-1, chans) for f, c in zip(first, big)], axis=0
            )[None]
        ]
        big = [count * sec_count for count in big]
        split = big[0]

    both = jnp.stack([rewards, prompt_ids.astype(jnp.float32)], axis=1)
    both = doubled_gather(both, "sec")
    all_rewards = both[:, 0]
    catalog = jnp.arange(prompt_count, dtype=jnp.int32)
    onehot = (both[:, 1].astype(jnp.int32)[:, None] == catalog[None, :]).astype(jnp.float32)
    own = (prompt_ids == catalog).astype(jnp.float32)
    advantage = advantages(onehot, own, all_rewards, rewards[0])

    key_rows = w_key.shape[0]
    tokens_up = -(-context_tokens // 16) * 16
    own_context = lax.dynamic_slice_in_dim(
        context, lax.axis_index("sec") * key_rows, key_rows, axis=2
    )
    own_context = jnp.pad(own_context, ((0, 0), (0, tokens_up - context_tokens), (0, 0)))
    partial = jnp.dot(
        own_context.reshape(prompt_count * tokens_up, key_rows),
        jnp.concatenate([w_key, w_value], axis=1),
        preferred_element_type=jnp.float32,
    ).reshape(prompt_count, tokens_up, 2 * col_piece)
    wanted = jnp.einsum(
        "ip,ptc->itc", onehot, partial, precision=lax.Precision.HIGHEST
    )
    own_part = halved_sum(wanted, "sec", jnp.bfloat16).astype(jnp.bfloat16)
    whole = doubled_gather(own_part, "dev").reshape(dev_count, tokens_up, 2, col_piece)
    whole = whole.transpose(2, 1, 0, 3).reshape(2, tokens_up, chans)
    lane = 2 * HEAD
    pairs = chans // lane
    valid = jnp.arange(tokens_up)[None, :, None] < context_tokens
    by_pair = jnp.where(valid, whole, 0).reshape(2, tokens_up, pairs, 2, HEAD)
    by_pair = jnp.pad(by_pair, ((0, 0), (0, lane - tokens_up), (0, 0), (0, 0), (0, 0)))
    eye = jnp.eye(2, dtype=jnp.bfloat16)
    key_blocks = (
        (by_pair[0] * (1.0 / math.sqrt(HEAD))).astype(jnp.bfloat16).transpose(1, 2, 3, 0)[
            :, :, :, None, :
        ]
        * eye[None, :, None, :, None]
    ).reshape(pairs, lane, 2 * lane)
    value_blocks = (
        by_pair[1].transpose(1, 2, 0, 3)[:, :, :, None, :] * eye[None, :, None, :, None]
    ).reshape(pairs, 2 * lane, lane)
    inside = (jnp.arange(lane) < context_tokens).astype(jnp.bfloat16)
    ones = jnp.broadcast_to(
        inside[None, :, None, None] * eye[:, None, :, None], (2, lane, 2, HEAD)
    ).reshape(1, 2 * lane, lane)
    value_blocks = jnp.concatenate(
        [value_blocks, jnp.broadcast_to(ones, value_blocks.shape)], axis=2
    )

    position = lax.axis_index("dev")
    flags = jnp.stack(
        [position > 0, position < dev_count - 1, lax.axis_index("sec"), position]
    ).astype(jnp.int32)
    planes = jnp.concatenate([latents, noise[:, 0]], axis=0)
    planes = to_tokens(with_halo(planes, "dev", 2, 2 * HALO))
    x, noise_wide = planes[0], planes[1:]
    plans = [plan(k) for k in range(STEPS)]
    factors = jnp.array([(s, b, g, b / g) for s, b, g in plans], jnp.float32)

    gains = jnp.stack([0.5 * gain_first, gain_second, 0.5 * gain_third])
    rest = (key_blocks, value_blocks, gains, in_full, final_full)
    gradient = jnp.zeros((feats, chans), jnp.float32)
    for first in range(0, STEPS, GROUP):
        if first:
            x = with_halo(x, "dev", 1, HALO * cols)
        part = slice(first, first + GROUP)
        x, share = run_steps(
            rows,
            cols,
            big,
            split,
            relative,
            flags,
            factors[part],
            sources,
            x,
            noise_wide[part],
            rest,
            time_bias[part],
        )
        gradient = gradient + share
    latent = from_tokens(x, rows, cols)[None]

    gradient = gradient * advantage
    row_piece = chans // sec_count
    arranged = gradient.reshape(dev_count, feats // dev_count, sec_count, row_piece)
    arranged = arranged.transpose(2, 0, 1, 3).reshape(sec_count * dev_count, -1)
    arrived = lax.all_to_all(arranged, ("sec", "dev"), split_axis=0, concat_axis=0, tiled=True)
    grad_shard = jnp.sum(arrived, axis=0).reshape(feats // dev_count, row_piece).T
    grad_shard = -grad_shard / sec_count
    moment_one = 0.9 * moment_first + 0.1 * grad_shard
    moment_two = 0.999 * moment_second + 0.001 * grad_shard * grad_shard
    new_weight = w_final - learn_rate * moment_one / (jnp.sqrt(moment_two) + 1e-08)
    return (latent, new_weight, moment_one, moment_two)


def solution(mesh):
    weight = P("sec", "dev")
    placed = (
        (P("sec", None, "dev", None), P(None, "sec", None, "dev", None), P("sec"), P("sec"))
        + (P(),) * 5
        + (weight,) * 9
    )
    return jax.shard_map(
        per_device,
        mesh=mesh,
        in_specs=placed,
        out_specs=(P("sec", None, "dev", None), weight, weight, weight),
        check_vma=False,
    )
```

```python
import functools
import math

import jax
import jax.numpy as jnp
from jax import lax
from jax.experimental import pallas as pl
from jax.experimental.pallas import tpu as pltpu
from jax.sharding import PartitionSpec as P

HEAD = 64
STEPS = 6
LANES = 128
GROUP = 3
HALO = 4
CHUNK_ROWS = 4

alpha_bars = (0.1, 0.15, 0.21, 0.28, 0.36, 0.45, 0.55)
norm_eps = 1e-06
learn_rate = 0.001


def plan(step_index):
    current = alpha_bars[step_index]
    following = alpha_bars[step_index + 1]
    sigma = math.sqrt((1.0 - following) / (1.0 - current)) * math.sqrt(1.0 - current / following)
    scale = math.sqrt(following / current)
    beta = math.sqrt(1.0 - following - sigma * sigma) - scale * math.sqrt(1.0 - current)
    return (scale, beta, sigma)


def swap(value, axis, mask):
    size = lax.axis_size(axis)
    return lax.ppermute(value, axis, [(i, i ^ mask) for i in range(size)])


def bit_of(axis, mask):
    return (lax.axis_index(axis) & mask) != 0


def doubled_gather(value, axis):
    mask = 1
    while mask < lax.axis_size(axis):
        other = swap(value, axis, mask)
        upper = bit_of(axis, mask)
        value = jnp.concatenate(
            [jnp.where(upper, other, value), jnp.where(upper, value, other)], axis=0
        )
        mask *= 2
    return value


def with_halo(shard, axis, dim, width):
    size, length = (lax.axis_size(axis), shard.shape[dim])
    up = [(i, i + 1) for i in range(size - 1)]
    down = [(j, i) for i, j in up]
    last = lax.slice_in_dim(shard, length - width, length, axis=dim)
    first = lax.slice_in_dim(shard, 0, width, axis=dim)
    before = lax.ppermute(last, axis, up)
    after = lax.ppermute(first, axis, down)
    return jnp.concatenate([before, shard, after], axis=dim)


def lane_order(breadth):
    half = breadth // 2
    lane = jnp.arange(breadth)
    return (lane[:, None] == (2 * (lane % half) + lane // half)[None, :]).astype(jnp.float32)


def to_tokens(latent):
    count, chans, height, breadth = latent.shape
    split = jnp.dot(latent, lane_order(breadth), precision=lax.Precision.HIGHEST)
    blocks = split.reshape(count, chans, height // 2, 2, 2, breadth // 2)
    return blocks.transpose(0, 1, 3, 4, 2, 5).reshape(
        count, chans * 4, height * breadth // 4
    )


def from_tokens(tokens, rows, cols):
    feats = tokens.shape[0]
    blocks = tokens.reshape(feats // 4, 2, 2, rows, cols).transpose(0, 3, 1, 2, 4)
    return jnp.dot(
        blocks.reshape(feats // 4, 2 * rows, 2 * cols),
        lane_order(2 * cols).T,
        precision=lax.Precision.HIGHEST,
    )


def rms_scale(values, gain):
    mean_square = jnp.mean(values * values, axis=-1, keepdims=True)
    return values * lax.rsqrt(mean_square + norm_eps) * gain


def silu_of_twice(values):
    return values + values * jnp.tanh(values)


def weight_copies(counts, split, relative, flags, refs, targets, sems):
    main, pieces = refs[0], refs[1:]
    copies = ([], [], [])

    def add(which, source, target):
        number = len(copies[which])
        copies[which].append(pltpu.make_async_copy(source, target, sems.at[which, number]))

    for part in range(main.shape[0]):
        offset = 0
        for which, (count, target) in enumerate(zip(counts, targets)):
            here = split if which == 0 else count
            add(
                which,
                main.at[part, pl.ds(offset, here)],
                target.at[pl.ds(part * count, here)],
            )
            offset += here
    for piece, places in zip(pieces, relative):
        for number, (sec, dev) in enumerate(places):
            length = piece.shape[1]
            row = (flags[2] ^ sec) * counts[0] + split + (flags[3] ^ dev) * length
            row = pl.multiple_of(row, 16)
            add(0, piece.at[number], targets[0].at[pl.ds(row, length)])
    return copies


def interleave(*tasks):
    tasks = list(tasks)
    while tasks:
        for task in list(tasks):
            try:
                next(task)
            except StopIteration:
                tasks.remove(task)


def steps_kernel(
    rows,
    cols,
    counts,
    split,
    relative,
    flags,
    factors,
    *refs,
):
    source_count = 1 + len(relative)
    sources = refs[:source_count]
    (
        x_in,
        noise,
        key_blocks,
        value_blocks,
        bias,
        gains,
        w_in,
        w_final,
        x_out,
        grad_out,
        w_conv,
        w_plus,
        w_query,
        w_attn,
        hidden,
        columns,
        state,
        narrow,
        queries,
        added,
        acts,
        sems,
    ) = refs[source_count:]
    group = bias.shape[0]
    feats, chans = w_in.shape
    copies = weight_copies(
        counts, split, relative, flags, sources, (w_conv, w_query, w_attn), sems
    )
    for some in copies:
        for copy in some:
            copy.start()
    state[...] = x_in[...]
    grad_out[...] = jnp.zeros_like(grad_out)
    pairs = key_blocks.shape[0]
    wide = 2 * HEAD
    size = CHUNK_ROWS * cols
    lane_token = lax.broadcasted_iota(jnp.int32, (1, size), 1)
    edge = 16
    near = lax.broadcasted_iota(jnp.int32, (edge, 1), 0)
    taps = 3 * chans

    def activate(step, start, first):
        hidden[pl.ds(first, CHUNK_ROWS // 2)] = (
            lax.dot_general(
                state[:, pl.ds(start, size)].astype(jnp.bfloat16),
                w_in[...],
                (((0,), (0,)), ((), ())),
                preferred_element_type=jnp.float32,
            )
            + bias[pl.ds(step, 1), :]
        ).reshape(CHUNK_ROWS // 2, 2, cols, chans)
        yield
        for row in range(CHUNK_ROWS):
            place = 2 * first + row
            inside = jnp.where(
                place < HALO, flags[0], jnp.where(place >= HALO + rows, flags[1], 1)
            ).astype(jnp.float32)
            scales = []
            for low in range(0, cols, edge):
                value = hidden[first + row // 2, row % 2, low : low + edge, :]
                mean_square = jnp.mean(value * value, axis=-1, keepdims=True)
                scales.append(lax.rsqrt(mean_square + norm_eps))
            scales = jnp.concatenate(scales, axis=0)
            at = (first + (row + 1) // 2, (row + 1) % 2)
            for low in range(0, chans, LANES):
                lanes = slice(low, low + LANES)
                value = hidden[first + row // 2, row % 2, :, lanes]
                act = silu_of_twice(value * scales * gains[0:1, lanes]) * inside
                left = pltpu.roll(act, 1, 0)
                right = pltpu.roll(act, cols - 1, 0)
                left = jnp.concatenate(
                    [jnp.where(near == 0, 0.0, left[:edge]), left[edge:]], axis=0
                )
                right = jnp.concatenate(
                    [right[: cols - edge], jnp.where(near == edge - 1, 0.0, right[cols - edge :])],
                    axis=0,
                )
                for which, piece in enumerate((left, act, right)):
                    columns[
                        at + (slice(None), pl.ds(which * chans + low, LANES))
                    ] = piece.astype(jnp.bfloat16)
            yield

    twos = (rows + HALO) // 4

    def convolve(part, carry):
        at = 1 + part * twos
        above, upper = columns[pl.ds(at, twos), 0], columns[pl.ds(at, twos), 1]
        lower, below = columns[pl.ds(at + 1, twos), 0], columns[pl.ds(at + 1, twos), 1]

        def product(value, weight):
            return jnp.dot(
                value.reshape(twos * cols, taps), weight, preferred_element_type=jnp.float32
            )

        plus = product(upper + lower, w_plus[...])
        minus = product(lower - upper, w_conv[taps : 2 * taps, :])
        span = pl.ds(at, twos)
        even = plus + minus + product(above - lower, w_conv[:taps, :])
        hidden[span, 0] += even.reshape(twos, cols, chans)
        odd = plus - minus - product(upper - below, w_conv[2 * taps :, :])
        hidden[span, 1] += odd.reshape(twos, cols, chans)
        return carry

    def finish(step, start):
        row_pair = lax.div(start, 2 * cols)

        def mixed_block(low):
            row = low // cols
            return hidden[row_pair + row // 2, row % 2, low % cols : low % cols + edge, :]

        for low in range(0, size, edge):
            value = rms_scale(mixed_block(low), gains[1:2, :])
            narrow[low : low + edge, :] = value.astype(jnp.bfloat16)
        yield
        queries[...] = jnp.dot(
            narrow[...], w_query[...], preferred_element_type=jnp.float32
        ).astype(jnp.bfloat16)
        yield
        for pair in range(pairs):
            lanes = slice(pair * wide, (pair + 1) * wide)
            scores = jnp.dot(
                queries[:, lanes], key_blocks[pair], preferred_element_type=jnp.float32
            )
            sums = jnp.dot(
                jnp.exp(scores).astype(jnp.bfloat16),
                value_blocks[pair],
                preferred_element_type=jnp.float32,
            )
            narrow[:, lanes] = (
                sums[:, :wide] * pl.reciprocal(sums[:, wide:], approx=True)
            ).astype(jnp.bfloat16)
            yield
        added[...] = jnp.dot(narrow[...], w_attn[...], preferred_element_type=jnp.float32)
        yield
        for low in range(0, size, edge):
            output = mixed_block(low) + added[low : low + edge, :]
            act = silu_of_twice(rms_scale(output, gains[2:3, :]))
            acts[low : low + edge, :] = act.astype(jnp.bfloat16)
        yield
        predicted = jnp.dot(acts[...], w_final[...], preferred_element_type=jnp.float32)
        span = pl.ds(start, size)
        noise_now = noise[step, :, span]
        state[:, span] = (
            factors[step, 0] * state[:, span]
            + factors[step, 1] * predicted.T
            + factors[step, 2] * noise_now
        )
        place = start + lane_token
        own = (place >= HALO * cols) & (place < (HALO + rows) * cols)
        weights = jnp.where(own, noise_now, 0.0)
        upper = weights.astype(jnp.bfloat16)
        lower = (weights - upper.astype(jnp.float32)).astype(jnp.bfloat16)
        share = jnp.dot(
            jnp.concatenate([upper, lower], axis=0), acts[...], preferred_element_type=jnp.float32
        )
        grad_out[...] += factors[step, 3] * (share[:feats] + share[feats:])

    chunks = state.shape[1] // size

    def fill(chunk, carry):
        interleave(activate(0, pl.multiple_of(chunk * size, size), chunk * (CHUNK_ROWS // 2)))
        return carry

    lax.fori_loop(0, chunks, fill, 0)
    for some in copies:
        for copy in some:
            copy.wait()
    block = chans // 5

    def combine(number, carry):
        here = pl.multiple_of(number * block, block)
        first, middle, final = (
            w_conv[pl.ds(tap * taps + here, block), :].astype(jnp.float32) for tap in range(3)
        )
        outer = 0.5 * (first + final)
        w_plus[pl.ds(here, block), :] = (outer + 0.5 * middle).astype(jnp.bfloat16)
        w_conv[pl.ds(taps + here, block), :] = (outer - 0.5 * middle).astype(jnp.bfloat16)
        return carry

    lax.fori_loop(0, taps // block, combine, 0)

    def one_step(step, carry):
        lax.fori_loop(0, 2, convolve, 0)
        last = step == group - 1
        base = jnp.where(last, HALO, HALO // 2) * cols
        count = jnp.where(last, chunks - 2, chunks - 1)
        after = jnp.minimum(step + 1, group - 1)

        def place(number):
            return pl.multiple_of(base + number * size, 2 * cols)

        def rest(number, carry):
            start = place(jnp.maximum(number - 1, 0))
            first = jnp.where(number == 0, state.shape[1] // (2 * cols), lax.div(start, 2 * cols))
            interleave(finish(step, place(number)), activate(after, start, first))
            return carry

        lax.fori_loop(0, count, rest, 0)

        @pl.when(step < group - 1)
        def _():
            start = place(count - 1)
            interleave(activate(after, start, lax.div(start, 2 * cols)))

        return carry

    lax.fori_loop(0, group, one_step, 0)
    x_out[...] = state[:, HALO * cols : (HALO + rows) * cols]


def run_steps(rows, cols, counts, split, relative, flags, factors, sources, x, noise, rest, bias):
    key_blocks, value_blocks, gains, w_in, w_final = rest
    feats, chans = w_in.shape
    tall_rows = rows + 2 * HALO
    vmem = pl.BlockSpec(memory_space=pltpu.VMEM)
    smem = pl.BlockSpec(memory_space=pltpu.SMEM)
    token_rows = sum(rows + 2 * k for k in range(GROUP)) * cols
    most = sources[0].shape[0] + sum(len(places) for places in relative)
    return pl.pallas_call(
        functools.partial(steps_kernel, rows, cols, counts, split, relative),
        out_shape=(
            jax.ShapeDtypeStruct((feats, rows * cols), jnp.float32),
            jax.ShapeDtypeStruct((feats, chans), jnp.float32),
        ),
        in_specs=[smem, smem]
        + [pl.BlockSpec(memory_space=pl.ANY)] * len(sources)
        + [vmem] * 8,
        out_specs=(vmem, vmem),
        scratch_shapes=[
            pltpu.VMEM((9 * chans, chans), jnp.bfloat16),
            pltpu.VMEM((3 * chans, chans), jnp.bfloat16),
            pltpu.VMEM((chans, chans), jnp.bfloat16),
            pltpu.VMEM((chans, chans), jnp.bfloat16),
            pltpu.VMEM(((tall_rows + CHUNK_ROWS) // 2, 2, cols, chans), jnp.float32),
            pltpu.VMEM(((tall_rows + CHUNK_ROWS) // 2 + 1, 2, cols, 3 * chans), jnp.bfloat16),
            pltpu.VMEM((feats, tall_rows * cols), jnp.float32),
            pltpu.VMEM((CHUNK_ROWS * cols, chans), jnp.bfloat16),
            pltpu.VMEM((CHUNK_ROWS * cols, chans), jnp.bfloat16),
            pltpu.VMEM((CHUNK_ROWS * cols, chans), jnp.float32),
            pltpu.VMEM((CHUNK_ROWS * cols, chans), jnp.bfloat16),
            pltpu.SemaphoreType.DMA((3, most)),
        ],
        compiler_params=pltpu.CompilerParams(vmem_limit_bytes=52 * 2**20),
        cost_estimate=pl.CostEstimate(
            flops=2 * token_rows * chans * chans * 12,
            bytes_accessed=12 * chans * chans * 2,
            transcendentals=4 * token_rows * chans,
        ),
    )(flags, factors, *sources, x, noise, key_blocks, value_blocks, bias, gains, w_in, w_final)


def advantages(onehot, own, rewards, own_reward):
    counts = jnp.sum(onehot, axis=0)
    sums = jnp.sum(onehot * rewards[:, None], axis=0)
    squares = jnp.sum(onehot * (rewards * rewards)[:, None], axis=0)
    safe_count = jnp.maximum(counts, 1.0)
    means = sums / safe_count
    spreads = jnp.sqrt(jnp.maximum(squares / safe_count - means * means, 1.0))
    own_mean = jnp.sum(own * means)
    own_spread = jnp.sum(own * spreads)
    return (own_reward - own_mean) / own_spread


def per_device(
    latents,
    noise,
    rewards,
    prompt_ids,
    context,
    time_bias,
    gain_first,
    gain_second,
    gain_third,
    w_in,
    w_conv,
    w_query,
    w_key,
    w_value,
    w_attn_out,
    w_final,
    moment_first,
    moment_second,
):
    sec_count = lax.axis_size("sec")
    dev_count = lax.axis_size("dev")
    prompt_count, context_tokens, _ = context.shape
    assert latents.shape[0] == 1
    col_piece = w_conv.shape[1]
    chans = col_piece * dev_count
    feats = w_in.shape[0] * sec_count
    rows, cols = latents.shape[2] // 2, latents.shape[3] // 2

    pieces = [
        w_conv,
        w_query,
        w_attn_out,
        w_in,
        w_final.astype(jnp.bfloat16).reshape(-1, col_piece),
    ]
    counts = [piece.shape[0] for piece in pieces]
    big = counts[:3]
    used = sum(counts)
    unit = 16 * dev_count
    padded = -(-used // unit) * unit
    whole_tiles = all(count % 16 == 0 for count in big)
    doubled = int(padded * 0.36) // unit * unit if whole_tiles else 0
    split = counts[0] - doubled
    pieces = [w_conv[:split]] + pieces[1:]
    pieces.append(jnp.zeros((padded - used, col_piece), jnp.bfloat16))
    blocks = [jnp.concatenate(pieces, axis=0), w_conv[split:]]
    main_length, length = (padded - doubled) // dev_count, doubled // dev_count
    block = jnp.concatenate([b.reshape(dev_count, -1, col_piece) for b in blocks], axis=1)
    block = block.reshape(padded, col_piece)
    block = lax.all_to_all(block, "dev", split_axis=0, concat_axis=1, tiled=True)
    packed = lax.all_gather(block[:main_length], ("sec", "dev"), axis=0, tiled=True)
    packed = packed.reshape(sec_count, padded - doubled, chans)
    sources, relative = [packed], []
    after = [jnp.float32(0), jnp.float32(0)]
    if doubled:
        turns = [("dev", 1 << k) for k in range(1, dev_count.bit_length() - 1)]
        turns += [("sec", 1 << k) for k in range(1, sec_count.bit_length() - 1)]
        turns += [("sec", 1), ("dev", 1)]
        held, places = [block[main_length:][None]], [((0, 0),)]
        for number, (axis, mask) in enumerate(turns):
            step = (mask, 0) if axis == "sec" else (0, mask)
            new = [swap(piece, axis, mask) for piece in held]
            new_places = [tuple((s ^ step[0], d ^ step[1]) for s, d in p) for p in places]
            if number < 2:
                after[number] = (new[0][0, 0, 0] * 0).astype(jnp.float32)
            if number < len(turns) - 2:
                held = [jnp.concatenate(held + new, axis=0)]
                places = [places[0] + new_places[0]]
            else:
                held, places = held + new, places + new_places
        sources, relative = sources + held, places

    at = split + counts[1] + counts[2]
    in_full = packed[:, at : at + counts[3]].reshape(feats, chans)
    at += counts[3]
    final_full = (
        packed[:, at : at + counts[4]]
        .reshape(sec_count, counts[4], dev_count, col_piece)
        .transpose(0, 2, 1, 3)
        .reshape(sec_count, dev_count, chans // sec_count, feats // dev_count)
        .transpose(0, 2, 1, 3)
        .reshape(chans, feats)
    )
    if not whole_tiles:
        first = [sum(big[:k]) for k in range(3)]
        sources = [
            jnp.concatenate(
                [packed[:, f : f + c].reshape(-1, chans) for f, c in zip(first, big)], axis=0
            )[None]
        ]
        big = [count * sec_count for count in big]
        split = big[0]

    both = jnp.stack([rewards, prompt_ids.astype(jnp.float32)], axis=1) + after[0]
    both = doubled_gather(both, "sec")
    all_rewards = both[:, 0]
    catalog = jnp.arange(prompt_count, dtype=jnp.int32)
    onehot = (both[:, 1].astype(jnp.int32)[:, None] == catalog[None, :]).astype(jnp.float32)
    own = (prompt_ids == catalog).astype(jnp.float32)
    advantage = advantages(onehot, own, all_rewards, rewards[0])

    key_rows = w_key.shape[0]
    tokens_up = -(-context_tokens // 16) * 16
    own_context = lax.dynamic_slice_in_dim(
        context, lax.axis_index("sec") * key_rows, key_rows, axis=2
    )
    own_context = jnp.pad(own_context, ((0, 0), (0, tokens_up - context_tokens), (0, 0)))
    partial = jnp.dot(
        own_context.reshape(prompt_count * tokens_up, key_rows),
        jnp.concatenate([w_key, w_value], axis=1),
        preferred_element_type=jnp.float32,
    ).reshape(prompt_count, tokens_up, 2 * col_piece)
    wanted = jnp.einsum(
        "ip,ptc->itc", onehot + after[1], partial, precision=lax.Precision.HIGHEST
    ).astype(jnp.bfloat16)
    arrived = lax.all_to_all(wanted, "sec", split_axis=0, concat_axis=0, tiled=True)
    own_part = jnp.sum(arrived.astype(jnp.float32), axis=0, keepdims=True).astype(jnp.bfloat16)
    whole = doubled_gather(own_part, "dev").reshape(dev_count, tokens_up, 2, col_piece)
    whole = whole.transpose(2, 1, 0, 3).reshape(2, tokens_up, chans)
    lane = 2 * HEAD
    pairs = chans // lane
    valid = jnp.arange(tokens_up)[None, :, None] < context_tokens
    by_pair = jnp.where(valid, whole, 0).reshape(2, tokens_up, pairs, 2, HEAD)
    by_pair = jnp.pad(by_pair, ((0, 0), (0, lane - tokens_up), (0, 0), (0, 0), (0, 0)))
    eye = jnp.eye(2, dtype=jnp.bfloat16)
    key_blocks = (
        (by_pair[0] * (1.0 / math.sqrt(HEAD))).astype(jnp.bfloat16).transpose(1, 2, 3, 0)[
            :, :, :, None, :
        ]
        * eye[None, :, None, :, None]
    ).reshape(pairs, lane, 2 * lane)
    value_blocks = (
        by_pair[1].transpose(1, 2, 0, 3)[:, :, :, None, :] * eye[None, :, None, :, None]
    ).reshape(pairs, 2 * lane, lane)
    inside = (jnp.arange(lane) < context_tokens).astype(jnp.bfloat16)
    ones = jnp.broadcast_to(
        inside[None, :, None, None] * eye[:, None, :, None], (2, lane, 2, HEAD)
    ).reshape(1, 2 * lane, lane)
    value_blocks = jnp.concatenate(
        [value_blocks, jnp.broadcast_to(ones, value_blocks.shape)], axis=2
    )

    position = lax.axis_index("dev")
    flags = jnp.stack(
        [position > 0, position < dev_count - 1, lax.axis_index("sec"), position]
    ).astype(jnp.int32)
    planes = jnp.concatenate([latents, noise[:, 0]], axis=0) + after[0]
    planes = to_tokens(with_halo(planes, "dev", 2, 2 * HALO))
    x, noise_wide = planes[0], planes[1:]
    plans = [plan(k) for k in range(STEPS)]
    factors = jnp.array([(s, b, g, b / g) for s, b, g in plans], jnp.float32)

    gains = jnp.stack([0.5 * gain_first, gain_second, 0.5 * gain_third])
    rest = (key_blocks, value_blocks, gains, in_full, final_full)
    gradient = jnp.zeros((feats, chans), jnp.float32)
    for first in range(0, STEPS, GROUP):
        if first:
            x = with_halo(x, "dev", 1, HALO * cols)
        part = slice(first, first + GROUP)
        x, share = run_steps(
            rows,
            cols,
            big,
            split,
            relative,
            flags,
            factors[part],
            sources,
            x,
            noise_wide[part],
            rest,
            time_bias[part],
        )
        gradient = gradient + share
    latent = from_tokens(x, rows, cols)[None]

    gradient = gradient * advantage
    row_piece = chans // sec_count
    arranged = gradient.reshape(dev_count, feats // dev_count, sec_count, row_piece)
    arranged = arranged.transpose(2, 0, 1, 3).reshape(sec_count * dev_count, -1)
    arrived = lax.all_to_all(arranged, ("sec", "dev"), split_axis=0, concat_axis=0, tiled=True)
    grad_shard = jnp.sum(arrived, axis=0).reshape(feats // dev_count, row_piece).T
    grad_shard = -grad_shard / sec_count
    moment_one = 0.9 * moment_first + 0.1 * grad_shard
    moment_two = 0.999 * moment_second + 0.001 * grad_shard * grad_shard
    new_weight = w_final - learn_rate * moment_one / (jnp.sqrt(moment_two) + 1e-08)
    return (latent, new_weight, moment_one, moment_two)


def solution(mesh):
    weight = P("sec", "dev")
    placed = (
        (P("sec", None, "dev", None), P(None, "sec", None, "dev", None), P("sec"), P("sec"))
        + (P(),) * 5
        + (weight,) * 9
    )
    return jax.shard_map(
        per_device,
        mesh=mesh,
        in_specs=placed,
        out_specs=(P("sec", None, "dev", None), weight, weight, weight),
        check_vma=False,
    )
```

```python
import functools
import math

import jax
import jax.numpy as jnp
from jax import lax
from jax.experimental import pallas as pl
from jax.experimental.pallas import tpu as pltpu
from jax.sharding import PartitionSpec as P

HEAD = 64
STEPS = 6
GROUP = 3
HALO = 4
CHUNK_ROWS = 4

alpha_bars = (0.1, 0.15, 0.21, 0.28, 0.36, 0.45, 0.55)
norm_eps = 1e-06
learn_rate = 0.001


def plan(step_index):
    current = alpha_bars[step_index]
    following = alpha_bars[step_index + 1]
    sigma = math.sqrt((1.0 - following) / (1.0 - current)) * math.sqrt(1.0 - current / following)
    scale = math.sqrt(following / current)
    beta = math.sqrt(1.0 - following - sigma * sigma) - scale * math.sqrt(1.0 - current)
    return (scale, beta, sigma)


def swap(value, axis, mask):
    size = lax.axis_size(axis)
    return lax.ppermute(value, axis, [(i, i ^ mask) for i in range(size)])


def bit_of(axis, mask):
    return (lax.axis_index(axis) & mask) != 0


def doubled_gather(value, axis):
    mask = 1
    while mask < lax.axis_size(axis):
        other = swap(value, axis, mask)
        upper = bit_of(axis, mask)
        value = jnp.concatenate(
            [jnp.where(upper, other, value), jnp.where(upper, value, other)], axis=0
        )
        mask *= 2
    return value


def with_halo(shard, axis, dim, width):
    size, length = (lax.axis_size(axis), shard.shape[dim])
    up = [(i, i + 1) for i in range(size - 1)]
    down = [(j, i) for i, j in up]
    last = lax.slice_in_dim(shard, length - width, length, axis=dim)
    first = lax.slice_in_dim(shard, 0, width, axis=dim)
    before = lax.ppermute(last, axis, up)
    after = lax.ppermute(first, axis, down)
    return jnp.concatenate([before, shard, after], axis=dim)


def lane_order(breadth):
    half = breadth // 2
    lane = jnp.arange(breadth)
    return (lane[:, None] == (2 * (lane % half) + lane // half)[None, :]).astype(jnp.float32)


def to_tokens(latent):
    count, chans, height, breadth = latent.shape
    split = jnp.dot(latent, lane_order(breadth), precision=lax.Precision.HIGHEST)
    blocks = split.reshape(count, chans, height // 2, 2, 2, breadth // 2)
    return blocks.transpose(0, 1, 3, 4, 2, 5).reshape(
        count, chans * 4, height * breadth // 4
    )


def from_tokens(tokens, rows, cols):
    feats = tokens.shape[0]
    blocks = tokens.reshape(feats // 4, 2, 2, rows, cols).transpose(0, 3, 1, 2, 4)
    return jnp.dot(
        blocks.reshape(feats // 4, 2 * rows, 2 * cols),
        lane_order(2 * cols).T,
        precision=lax.Precision.HIGHEST,
    )


def rms_scale(values, gain):
    mean_square = jnp.mean(values * values, axis=-1, keepdims=True)
    return values * lax.rsqrt(mean_square + norm_eps) * gain


def silu_of_twice(values):
    return values + values * jnp.tanh(values)


def weight_copies(counts, split, relative, flags, refs, targets, sems):
    main, pieces = refs[0], refs[1:]
    copies = ([], [], [])

    def add(which, source, target):
        number = len(copies[which])
        copies[which].append(pltpu.make_async_copy(source, target, sems.at[which, number]))

    for part in range(main.shape[0]):
        offset = 0
        for which, (count, target) in enumerate(zip(counts, targets)):
            here = split if which == 0 else count
            add(
                which,
                main.at[part, pl.ds(offset, here)],
                target.at[pl.ds(part * count, here)],
            )
            offset += here
    for piece, places in zip(pieces, relative):
        for number, (sec, dev) in enumerate(places):
            length = piece.shape[1]
            row = (flags[2] ^ sec) * counts[0] + split + (flags[3] ^ dev) * length
            row = pl.multiple_of(row, 16)
            add(0, piece.at[number], targets[0].at[pl.ds(row, length)])
    return copies


def interleave(*tasks):
    tasks = list(tasks)
    while tasks:
        for task in list(tasks):
            try:
                next(task)
            except StopIteration:
                tasks.remove(task)


def steps_kernel(
    rows,
    cols,
    counts,
    split,
    relative,
    flags,
    factors,
    *refs,
):
    source_count = 1 + len(relative)
    sources = refs[:source_count]
    (
        x_in,
        noise,
        key_blocks,
        value_blocks,
        bias,
        gains,
        w_in,
        w_final,
        x_out,
        grad_out,
        w_conv,
        w_plus,
        w_query,
        w_attn,
        hidden,
        columns,
        state,
        sems,
    ) = refs[source_count:]
    group = bias.shape[0]
    feats, chans = w_in.shape
    copies = weight_copies(
        counts, split, relative, flags, sources, (w_conv, w_query, w_attn), sems
    )
    for some in copies:
        for copy in some:
            copy.start()
    state[...] = x_in[...]
    grad_out[...] = jnp.zeros_like(grad_out)
    pairs = key_blocks.shape[0]
    wide = 2 * HEAD
    size = CHUNK_ROWS * cols
    lane_token = lax.broadcasted_iota(jnp.int32, (1, size), 1)
    edge = 16
    near = lax.broadcasted_iota(jnp.int32, (edge, 1), 0)
    taps = 3 * chans

    def activate(step, start):
        before_norm = (
            lax.dot_general(
                state[:, pl.ds(start, size)].astype(jnp.bfloat16),
                w_in[...],
                (((0,), (0,)), ((), ())),
                preferred_element_type=jnp.float32,
            )
            + bias[pl.ds(step, 1), :]
        )
        first = lax.div(start, 2 * cols)
        yield
        for row in range(CHUNK_ROWS):
            value = before_norm[row * cols : (row + 1) * cols]
            hidden[first + row // 2, row % 2] = value
            act = silu_of_twice(rms_scale(value, gains[0:1, :]))
            place = 2 * first + row
            inside = jnp.where(
                place < HALO, flags[0], jnp.where(place >= HALO + rows, flags[1], 1)
            )
            act = act * inside.astype(jnp.float32)
            at = (first + (row + 1) // 2, (row + 1) % 2)
            left = pltpu.roll(act, 1, 0)
            right = pltpu.roll(act, cols - 1, 0)
            first_left = jnp.where(near == 0, 0.0, left[:edge])
            last_right = jnp.where(near == edge - 1, 0.0, right[cols - edge :])
            columns[at + (slice(0, edge), slice(0, chans))] = first_left.astype(jnp.bfloat16)
            columns[at + (slice(edge, cols), slice(0, chans))] = left[edge:].astype(jnp.bfloat16)
            columns[at + (slice(0, cols), slice(chans, 2 * chans))] = act.astype(jnp.bfloat16)
            columns[at + (slice(0, cols - edge), slice(2 * chans, taps))] = right[
                : cols - edge
            ].astype(jnp.bfloat16)
            columns[at + (slice(cols - edge, cols), slice(2 * chans, taps))] = last_right.astype(
                jnp.bfloat16
            )
            yield

    twos = (rows + HALO) // 4

    def convolve(part, carry):
        at = 1 + part * twos
        above, upper = columns[pl.ds(at, twos), 0], columns[pl.ds(at, twos), 1]
        lower, below = columns[pl.ds(at + 1, twos), 0], columns[pl.ds(at + 1, twos), 1]

        def product(value, weight):
            return jnp.dot(
                value.reshape(twos * cols, taps), weight, preferred_element_type=jnp.float32
            )

        plus = product(upper + lower, w_plus[...])
        minus = product(lower - upper, w_conv[taps : 2 * taps, :])
        span = pl.ds(at, twos)
        even = plus + minus + product(above - lower, w_conv[:taps, :])
        hidden[span, 0] += even.reshape(twos, cols, chans)
        odd = plus - minus - product(upper - below, w_conv[2 * taps :, :])
        hidden[span, 1] += odd.reshape(twos, cols, chans)
        return carry

    def finish(step, start):
        row_pair = lax.div(start, 2 * cols)
        mixed = hidden[pl.ds(row_pair, CHUNK_ROWS // 2)].reshape(size, chans)
        normed = rms_scale(mixed, gains[1:2, :]).astype(jnp.bfloat16)
        yield
        queries = jnp.dot(normed, w_query[...], preferred_element_type=jnp.float32).astype(
            jnp.bfloat16
        )
        yield
        heads = []
        for pair in range(pairs):
            scores = jnp.dot(
                queries[:, pair * wide : (pair + 1) * wide],
                key_blocks[pair],
                preferred_element_type=jnp.float32,
            )
            sums = jnp.dot(
                jnp.exp(scores).astype(jnp.bfloat16),
                value_blocks[pair],
                preferred_element_type=jnp.float32,
            )
            heads.append(
                (sums[:, :wide] * pl.reciprocal(sums[:, wide:], approx=True)).astype(
                    jnp.bfloat16
                )
            )
            yield
        attended = jnp.concatenate(heads, axis=1)
        output = mixed + jnp.dot(attended, w_attn[...], preferred_element_type=jnp.float32)
        act = silu_of_twice(rms_scale(output, gains[2:3, :])).astype(jnp.bfloat16)
        predicted = jnp.dot(act, w_final[...], preferred_element_type=jnp.float32)
        span = pl.ds(start, size)
        noise_now = noise[step, :, span]
        state[:, span] = (
            factors[step, 0] * state[:, span]
            + factors[step, 1] * predicted.T
            + factors[step, 2] * noise_now
        )
        place = start + lane_token
        own = (place >= HALO * cols) & (place < (HALO + rows) * cols)
        weights = jnp.where(own, noise_now, 0.0)
        upper = weights.astype(jnp.bfloat16)
        lower = (weights - upper.astype(jnp.float32)).astype(jnp.bfloat16)
        share = jnp.dot(
            jnp.concatenate([upper, lower], axis=0), act, preferred_element_type=jnp.float32
        )
        grad_out[...] += factors[step, 3] * (share[:feats] + share[feats:])

    chunks = state.shape[1] // size

    def fill(chunk, carry):
        interleave(activate(0, pl.multiple_of(chunk * size, size)))
        return carry

    lax.fori_loop(0, chunks, fill, 0)
    for some in copies:
        for copy in some:
            copy.wait()
    block = chans // 5

    def combine(number, carry):
        here = pl.multiple_of(number * block, block)
        first, middle, final = (
            w_conv[pl.ds(tap * taps + here, block), :].astype(jnp.float32) for tap in range(3)
        )
        outer = 0.5 * (first + final)
        w_plus[pl.ds(here, block), :] = (outer + 0.5 * middle).astype(jnp.bfloat16)
        w_conv[pl.ds(taps + here, block), :] = (outer - 0.5 * middle).astype(jnp.bfloat16)
        return carry

    lax.fori_loop(0, taps // block, combine, 0)

    def one_step(step, carry):
        lax.fori_loop(0, 2, convolve, 0)
        last = step == group - 1
        base = jnp.where(last, HALO, HALO // 2) * cols
        count = jnp.where(last, chunks - 2, chunks - 1)
        after = jnp.minimum(step + 1, group - 1)

        def place(number):
            return pl.multiple_of(base + number * size, 2 * cols)

        def rest(number, carry):
            interleave(
                finish(step, place(number)), activate(after, place(jnp.maximum(number - 1, 0)))
            )
            return carry

        lax.fori_loop(0, count, rest, 0)

        @pl.when(step < group - 1)
        def _():
            interleave(activate(after, place(count - 1)))

        return carry

    lax.fori_loop(0, group, one_step, 0)
    x_out[...] = state[:, HALO * cols : (HALO + rows) * cols]


def run_steps(rows, cols, counts, split, relative, flags, factors, sources, x, noise, rest, bias):
    key_blocks, value_blocks, gains, w_in, w_final = rest
    feats, chans = w_in.shape
    tall_rows = rows + 2 * HALO
    vmem = pl.BlockSpec(memory_space=pltpu.VMEM)
    smem = pl.BlockSpec(memory_space=pltpu.SMEM)
    token_rows = sum(rows + 2 * k for k in range(GROUP)) * cols
    most = sources[0].shape[0] + sum(len(places) for places in relative)
    return pl.pallas_call(
        functools.partial(steps_kernel, rows, cols, counts, split, relative),
        out_shape=(
            jax.ShapeDtypeStruct((feats, rows * cols), jnp.float32),
            jax.ShapeDtypeStruct((feats, chans), jnp.float32),
        ),
        in_specs=[smem, smem]
        + [pl.BlockSpec(memory_space=pl.ANY)] * len(sources)
        + [vmem] * 8,
        out_specs=(vmem, vmem),
        scratch_shapes=[
            pltpu.VMEM((9 * chans, chans), jnp.bfloat16),
            pltpu.VMEM((3 * chans, chans), jnp.bfloat16),
            pltpu.VMEM((chans, chans), jnp.bfloat16),
            pltpu.VMEM((chans, chans), jnp.bfloat16),
            pltpu.VMEM((tall_rows // 2, 2, cols, chans), jnp.float32),
            pltpu.VMEM((tall_rows // 2 + 1, 2, cols, 3 * chans), jnp.bfloat16),
            pltpu.VMEM((feats, tall_rows * cols), jnp.float32),
            pltpu.SemaphoreType.DMA((3, most)),
        ],
        compiler_params=pltpu.CompilerParams(vmem_limit_bytes=52 * 2**20),
        cost_estimate=pl.CostEstimate(
            flops=2 * token_rows * chans * chans * 12,
            bytes_accessed=12 * chans * chans * 2,
            transcendentals=4 * token_rows * chans,
        ),
    )(flags, factors, *sources, x, noise, key_blocks, value_blocks, bias, gains, w_in, w_final)


def advantages(onehot, own, rewards, own_reward):
    counts = jnp.sum(onehot, axis=0)
    sums = jnp.sum(onehot * rewards[:, None], axis=0)
    squares = jnp.sum(onehot * (rewards * rewards)[:, None], axis=0)
    safe_count = jnp.maximum(counts, 1.0)
    means = sums / safe_count
    spreads = jnp.sqrt(jnp.maximum(squares / safe_count - means * means, 1.0))
    own_mean = jnp.sum(own * means)
    own_spread = jnp.sum(own * spreads)
    return (own_reward - own_mean) / own_spread


def per_device(
    latents,
    noise,
    rewards,
    prompt_ids,
    context,
    time_bias,
    gain_first,
    gain_second,
    gain_third,
    w_in,
    w_conv,
    w_query,
    w_key,
    w_value,
    w_attn_out,
    w_final,
    moment_first,
    moment_second,
):
    sec_count = lax.axis_size("sec")
    dev_count = lax.axis_size("dev")
    prompt_count, context_tokens, _ = context.shape
    assert latents.shape[0] == 1
    col_piece = w_conv.shape[1]
    chans = col_piece * dev_count
    feats = w_in.shape[0] * sec_count
    rows, cols = latents.shape[2] // 2, latents.shape[3] // 2

    pieces = [
        w_conv,
        w_query,
        w_attn_out,
        w_in,
        w_final.astype(jnp.bfloat16).reshape(-1, col_piece),
    ]
    counts = [piece.shape[0] for piece in pieces]
    big = counts[:3]
    used = sum(counts)
    unit = 16 * dev_count
    padded = -(-used // unit) * unit
    whole_tiles = all(count % 16 == 0 for count in big)
    split = counts[0]
    pieces.append(jnp.zeros((padded - used, col_piece), jnp.bfloat16))
    block = jnp.concatenate(pieces, axis=0)
    block = lax.all_to_all(block, "dev", split_axis=0, concat_axis=1, tiled=True)
    packed = lax.all_gather(block, ("sec", "dev"), axis=0, tiled=True)
    packed = packed.reshape(sec_count, padded, chans)
    sources, relative = [packed], []
    at = split + counts[1] + counts[2]
    in_full = packed[:, at : at + counts[3]].reshape(feats, chans)
    at += counts[3]
    final_full = (
        packed[:, at : at + counts[4]]
        .reshape(sec_count, counts[4], dev_count, col_piece)
        .transpose(0, 2, 1, 3)
        .reshape(sec_count, dev_count, chans // sec_count, feats // dev_count)
        .transpose(0, 2, 1, 3)
        .reshape(chans, feats)
    )
    if not whole_tiles:
        first = [sum(big[:k]) for k in range(3)]
        sources = [
            jnp.concatenate(
                [packed[:, f : f + c].reshape(-1, chans) for f, c in zip(first, big)], axis=0
            )[None]
        ]
        big = [count * sec_count for count in big]
        split = big[0]

    both = jnp.stack([rewards, prompt_ids.astype(jnp.float32)], axis=1)
    both = doubled_gather(both, "sec")
    all_rewards = both[:, 0]
    catalog = jnp.arange(prompt_count, dtype=jnp.int32)
    onehot = (both[:, 1].astype(jnp.int32)[:, None] == catalog[None, :]).astype(jnp.float32)
    own = (prompt_ids == catalog).astype(jnp.float32)
    advantage = advantages(onehot, own, all_rewards, rewards[0])

    key_rows = w_key.shape[0]
    tokens_up = -(-context_tokens // 16) * 16
    own_context = lax.dynamic_slice_in_dim(
        context, lax.axis_index("sec") * key_rows, key_rows, axis=2
    )
    own_context = jnp.pad(own_context, ((0, 0), (0, tokens_up - context_tokens), (0, 0)))
    partial = jnp.dot(
        own_context.reshape(prompt_count * tokens_up, key_rows),
        jnp.concatenate([w_key, w_value], axis=1),
        preferred_element_type=jnp.float32,
    ).reshape(prompt_count, tokens_up, 2 * col_piece)
    wanted = jnp.einsum(
        "ip,ptc->itc", onehot, partial, precision=lax.Precision.HIGHEST
    ).astype(jnp.bfloat16)
    arrived = lax.all_to_all(wanted, "sec", split_axis=0, concat_axis=0, tiled=True)
    own_part = jnp.sum(arrived.astype(jnp.float32), axis=0, keepdims=True).astype(jnp.bfloat16)
    whole = doubled_gather(own_part, "dev").reshape(dev_count, tokens_up, 2, col_piece)
    whole = whole.transpose(2, 1, 0, 3).reshape(2, tokens_up, chans)
    lane = 2 * HEAD
    pairs = chans // lane
    valid = jnp.arange(tokens_up)[None, :, None] < context_tokens
    by_pair = jnp.where(valid, whole, 0).reshape(2, tokens_up, pairs, 2, HEAD)
    by_pair = jnp.pad(by_pair, ((0, 0), (0, lane - tokens_up), (0, 0), (0, 0), (0, 0)))
    eye = jnp.eye(2, dtype=jnp.bfloat16)
    key_blocks = (
        (by_pair[0] * (1.0 / math.sqrt(HEAD))).astype(jnp.bfloat16).transpose(1, 2, 3, 0)[
            :, :, :, None, :
        ]
        * eye[None, :, None, :, None]
    ).reshape(pairs, lane, 2 * lane)
    value_blocks = (
        by_pair[1].transpose(1, 2, 0, 3)[:, :, :, None, :] * eye[None, :, None, :, None]
    ).reshape(pairs, 2 * lane, lane)
    inside = (jnp.arange(lane) < context_tokens).astype(jnp.bfloat16)
    ones = jnp.broadcast_to(
        inside[None, :, None, None] * eye[:, None, :, None], (2, lane, 2, HEAD)
    ).reshape(1, 2 * lane, lane)
    value_blocks = jnp.concatenate(
        [value_blocks, jnp.broadcast_to(ones, value_blocks.shape)], axis=2
    )

    position = lax.axis_index("dev")
    flags = jnp.stack(
        [position > 0, position < dev_count - 1, lax.axis_index("sec"), position]
    ).astype(jnp.int32)
    planes = jnp.concatenate([latents, noise[:, 0]], axis=0)
    planes = to_tokens(with_halo(planes, "dev", 2, 2 * HALO))
    x, noise_wide = planes[0], planes[1:]
    plans = [plan(k) for k in range(STEPS)]
    factors = jnp.array([(s, b, g, b / g) for s, b, g in plans], jnp.float32)

    gains = jnp.stack([0.5 * gain_first, gain_second, 0.5 * gain_third])
    rest = (key_blocks, value_blocks, gains, in_full, final_full)
    gradient = jnp.zeros((feats, chans), jnp.float32)
    for first in range(0, STEPS, GROUP):
        if first:
            x = with_halo(x, "dev", 1, HALO * cols)
        part = slice(first, first + GROUP)
        x, share = run_steps(
            rows,
            cols,
            big,
            split,
            relative,
            flags,
            factors[part],
            sources,
            x,
            noise_wide[part],
            rest,
            time_bias[part],
        )
        gradient = gradient + share
    latent = from_tokens(x, rows, cols)[None]

    gradient = gradient * advantage
    row_piece = chans // sec_count
    arranged = gradient.reshape(dev_count, feats // dev_count, sec_count, row_piece)
    arranged = arranged.transpose(2, 0, 1, 3).reshape(sec_count * dev_count, -1)
    arrived = lax.all_to_all(arranged, ("sec", "dev"), split_axis=0, concat_axis=0, tiled=True)
    grad_shard = jnp.sum(arrived, axis=0).reshape(feats // dev_count, row_piece).T
    grad_shard = -grad_shard / sec_count
    moment_one = 0.9 * moment_first + 0.1 * grad_shard
    moment_two = 0.999 * moment_second + 0.001 * grad_shard * grad_shard
    new_weight = w_final - learn_rate * moment_one / (jnp.sqrt(moment_two) + 1e-08)
    return (latent, new_weight, moment_one, moment_two)


def solution(mesh):
    weight = P("sec", "dev")
    placed = (
        (P("sec", None, "dev", None), P(None, "sec", None, "dev", None), P("sec"), P("sec"))
        + (P(),) * 5
        + (weight,) * 9
    )
    return jax.shard_map(
        per_device,
        mesh=mesh,
        in_specs=placed,
        out_specs=(P("sec", None, "dev", None), weight, weight, weight),
        check_vma=False,
    )
```

```python
import functools
import math

import jax
import jax.numpy as jnp
from jax import lax
from jax.experimental import pallas as pl
from jax.experimental.pallas import tpu as pltpu
from jax.sharding import PartitionSpec as P

HEAD = 64
STEPS = 6
GROUP = 3
HALO = 4
CHUNK_ROWS = 4

alpha_bars = (0.1, 0.15, 0.21, 0.28, 0.36, 0.45, 0.55)
norm_eps = 1e-06
learn_rate = 0.001


def plan(step_index):
    current = alpha_bars[step_index]
    following = alpha_bars[step_index + 1]
    sigma = math.sqrt((1.0 - following) / (1.0 - current)) * math.sqrt(1.0 - current / following)
    scale = math.sqrt(following / current)
    beta = math.sqrt(1.0 - following - sigma * sigma) - scale * math.sqrt(1.0 - current)
    return (scale, beta, sigma)


def swap(value, axis, mask):
    size = lax.axis_size(axis)
    return lax.ppermute(value, axis, [(i, i ^ mask) for i in range(size)])


def bit_of(axis, mask):
    return (lax.axis_index(axis) & mask) != 0


def doubled_gather(value, axis):
    mask = 1
    while mask < lax.axis_size(axis):
        other = swap(value, axis, mask)
        upper = bit_of(axis, mask)
        value = jnp.concatenate(
            [jnp.where(upper, other, value), jnp.where(upper, value, other)], axis=0
        )
        mask *= 2
    return value


def with_halo(shard, axis, dim, width):
    size, length = (lax.axis_size(axis), shard.shape[dim])
    up = [(i, i + 1) for i in range(size - 1)]
    down = [(j, i) for i, j in up]
    last = lax.slice_in_dim(shard, length - width, length, axis=dim)
    first = lax.slice_in_dim(shard, 0, width, axis=dim)
    before = lax.ppermute(last, axis, up)
    after = lax.ppermute(first, axis, down)
    return jnp.concatenate([before, shard, after], axis=dim)


def lane_order(breadth):
    half = breadth // 2
    lane = jnp.arange(breadth)
    return (lane[:, None] == (2 * (lane % half) + lane // half)[None, :]).astype(jnp.float32)


def to_tokens(latent):
    count, chans, height, breadth = latent.shape
    split = jnp.dot(latent, lane_order(breadth), precision=lax.Precision.HIGHEST)
    blocks = split.reshape(count, chans, height // 2, 2, 2, breadth // 2)
    return blocks.transpose(0, 1, 3, 4, 2, 5).reshape(
        count, chans * 4, height * breadth // 4
    )


def from_tokens(tokens, rows, cols):
    feats = tokens.shape[0]
    blocks = tokens.reshape(feats // 4, 2, 2, rows, cols).transpose(0, 3, 1, 2, 4)
    return jnp.dot(
        blocks.reshape(feats // 4, 2 * rows, 2 * cols),
        lane_order(2 * cols).T,
        precision=lax.Precision.HIGHEST,
    )


def rms_scale(values, gain):
    mean_square = jnp.mean(values * values, axis=-1, keepdims=True)
    return values * lax.rsqrt(mean_square + norm_eps) * gain


def silu_of_twice(values):
    return values + values * jnp.tanh(values)


def weight_copies(counts, split, relative, flags, refs, targets, sems):
    main, pieces = refs[0], refs[1:]
    copies = ([], [], [])

    def add(which, source, target):
        number = len(copies[which])
        copies[which].append(pltpu.make_async_copy(source, target, sems.at[which, number]))

    for part in range(main.shape[0]):
        offset = 0
        for which, (count, target) in enumerate(zip(counts, targets)):
            here = split if which == 0 else count
            add(
                which,
                main.at[part, pl.ds(offset, here)],
                target.at[pl.ds(part * count, here)],
            )
            offset += here
    for piece, places in zip(pieces, relative):
        for number, (sec, dev) in enumerate(places):
            length = piece.shape[1]
            row = (flags[2] ^ sec) * counts[0] + split + (flags[3] ^ dev) * length
            row = pl.multiple_of(row, 16)
            add(0, piece.at[number], targets[0].at[pl.ds(row, length)])
    return copies


def interleave(*tasks):
    tasks = list(tasks)
    while tasks:
        for task in list(tasks):
            try:
                next(task)
            except StopIteration:
                tasks.remove(task)


def steps_kernel(
    rows,
    cols,
    counts,
    split,
    relative,
    flags,
    factors,
    *refs,
):
    source_count = 1 + len(relative)
    sources = refs[:source_count]
    (
        x_in,
        noise,
        key_blocks,
        value_blocks,
        bias,
        gains,
        w_in,
        w_final,
        x_out,
        grad_out,
        w_conv,
        w_plus,
        w_query,
        w_attn,
        hidden,
        columns,
        state,
        sems,
    ) = refs[source_count:]
    group = bias.shape[0]
    feats, chans = w_in.shape
    copies = weight_copies(
        counts, split, relative, flags, sources, (w_conv, w_query, w_attn), sems
    )
    for some in copies:
        for copy in some:
            copy.start()
    state[...] = x_in[...]
    grad_out[...] = jnp.zeros_like(grad_out)
    pairs = key_blocks.shape[0]
    wide = 2 * HEAD
    size = CHUNK_ROWS * cols
    lane_token = lax.broadcasted_iota(jnp.int32, (1, size), 1)
    edge = 16
    near = lax.broadcasted_iota(jnp.int32, (edge, 1), 0)
    taps = 3 * chans

    def activate(step, start):
        before_norm = (
            lax.dot_general(
                state[:, pl.ds(start, size)].astype(jnp.bfloat16),
                w_in[...],
                (((0,), (0,)), ((), ())),
                preferred_element_type=jnp.float32,
            )
            + bias[pl.ds(step, 1), :]
        )
        first = lax.div(start, 2 * cols)
        yield
        for row in range(CHUNK_ROWS):
            value = before_norm[row * cols : (row + 1) * cols]
            hidden[first + row // 2, row % 2] = value
            act = silu_of_twice(rms_scale(value, gains[0:1, :]))
            place = 2 * first + row
            inside = jnp.where(
                place < HALO, flags[0], jnp.where(place >= HALO + rows, flags[1], 1)
            )
            act = act * inside.astype(jnp.float32)
            at = (first + (row + 1) // 2, (row + 1) % 2)
            left = pltpu.roll(act, 1, 0)
            right = pltpu.roll(act, cols - 1, 0)
            first_left = jnp.where(near == 0, 0.0, left[:edge])
            last_right = jnp.where(near == edge - 1, 0.0, right[cols - edge :])
            columns[at + (slice(0, edge), slice(0, chans))] = first_left.astype(jnp.bfloat16)
            columns[at + (slice(edge, cols), slice(0, chans))] = left[edge:].astype(jnp.bfloat16)
            columns[at + (slice(0, cols), slice(chans, 2 * chans))] = act.astype(jnp.bfloat16)
            columns[at + (slice(0, cols - edge), slice(2 * chans, taps))] = right[
                : cols - edge
            ].astype(jnp.bfloat16)
            columns[at + (slice(cols - edge, cols), slice(2 * chans, taps))] = last_right.astype(
                jnp.bfloat16
            )
            yield

    twos = (rows + HALO) // 4

    def convolve(part, carry):
        at = 1 + part * twos
        above, upper = columns[pl.ds(at, twos), 0], columns[pl.ds(at, twos), 1]
        lower, below = columns[pl.ds(at + 1, twos), 0], columns[pl.ds(at + 1, twos), 1]

        def product(value, weight):
            return jnp.dot(
                value.reshape(twos * cols, taps), weight, preferred_element_type=jnp.float32
            )

        plus = product(upper + lower, w_plus[...])
        minus = product(lower - upper, w_conv[taps : 2 * taps, :])
        span = pl.ds(at, twos)
        even = plus + minus + product(above - lower, w_conv[:taps, :])
        hidden[span, 0] += even.reshape(twos, cols, chans)
        odd = plus - minus - product(upper - below, w_conv[2 * taps :, :])
        hidden[span, 1] += odd.reshape(twos, cols, chans)
        return carry

    def finish(step, start):
        row_pair = lax.div(start, 2 * cols)
        mixed = hidden[pl.ds(row_pair, CHUNK_ROWS // 2)].reshape(size, chans)
        normed = rms_scale(mixed, gains[1:2, :]).astype(jnp.bfloat16)
        yield
        queries = jnp.dot(normed, w_query[...], preferred_element_type=jnp.float32).astype(
            jnp.bfloat16
        )
        yield
        heads = []
        for pair in range(pairs):
            scores = jnp.dot(
                queries[:, pair * wide : (pair + 1) * wide],
                key_blocks[pair],
                preferred_element_type=jnp.float32,
            )
            sums = jnp.dot(
                jnp.exp(scores).astype(jnp.bfloat16),
                value_blocks[pair],
                preferred_element_type=jnp.float32,
            )
            heads.append(
                (sums[:, :wide] * pl.reciprocal(sums[:, wide:], approx=True)).astype(
                    jnp.bfloat16
                )
            )
            yield
        attended = jnp.concatenate(heads, axis=1)
        output = mixed + jnp.dot(attended, w_attn[...], preferred_element_type=jnp.float32)
        act = silu_of_twice(rms_scale(output, gains[2:3, :])).astype(jnp.bfloat16)
        predicted = jnp.dot(act, w_final[...], preferred_element_type=jnp.float32)
        span = pl.ds(start, size)
        noise_now = noise[flags[4] + step, :, span]
        state[:, span] = (
            factors[step, 0] * state[:, span]
            + factors[step, 1] * predicted.T
            + factors[step, 2] * noise_now
        )
        place = start + lane_token
        own = (place >= HALO * cols) & (place < (HALO + rows) * cols)
        weights = jnp.where(own, noise_now, 0.0)
        upper = weights.astype(jnp.bfloat16)
        lower = (weights - upper.astype(jnp.float32)).astype(jnp.bfloat16)
        share = jnp.dot(
            jnp.concatenate([upper, lower], axis=0), act, preferred_element_type=jnp.float32
        )
        grad_out[...] += factors[step, 3] * (share[:feats] + share[feats:])

    chunks = state.shape[1] // size

    def fill(chunk, carry):
        interleave(activate(0, pl.multiple_of(chunk * size, size)))
        return carry

    lax.fori_loop(0, chunks, fill, 0)
    for some in copies:
        for copy in some:
            copy.wait()
    block = chans // 5

    def combine(number, carry):
        here = pl.multiple_of(number * block, block)
        first, middle, final = (
            w_conv[pl.ds(tap * taps + here, block), :].astype(jnp.float32) for tap in range(3)
        )
        outer = 0.5 * (first + final)
        w_plus[pl.ds(here, block), :] = (outer + 0.5 * middle).astype(jnp.bfloat16)
        w_conv[pl.ds(taps + here, block), :] = (outer - 0.5 * middle).astype(jnp.bfloat16)
        return carry

    lax.fori_loop(0, taps // block, combine, 0)

    def one_step(step, carry):
        lax.fori_loop(0, 2, convolve, 0)
        last = step == group - 1
        base = jnp.where(last, HALO, HALO // 2) * cols
        count = jnp.where(last, chunks - 2, chunks - 1)
        after = jnp.minimum(step + 1, group - 1)

        def place(number):
            return pl.multiple_of(base + number * size, 2 * cols)

        def beside(number, carry):
            interleave(finish(step, place(number)), activate(after, place(number - 1)))
            return carry

        def alone(number, carry):
            interleave(finish(step, place(number)))
            return carry

        lax.fori_loop(0, jnp.where(last, count, 1), alone, 0)

        @pl.when(step < group - 1)
        def _():
            lax.fori_loop(1, count, beside, 0)
            interleave(activate(after, place(count - 1)))

        return carry

    lax.fori_loop(0, group, one_step, 0)
    x_out[...] = state[:, HALO * cols : (HALO + rows) * cols]


def run_steps(rows, cols, counts, split, relative, flags, factors, sources, x, noise, rest, bias):
    key_blocks, value_blocks, gains, w_in, w_final = rest
    feats, chans = w_in.shape
    tall_rows = rows + 2 * HALO
    vmem = pl.BlockSpec(memory_space=pltpu.VMEM)
    smem = pl.BlockSpec(memory_space=pltpu.SMEM)
    token_rows = sum(rows + 2 * k for k in range(GROUP)) * cols
    most = sources[0].shape[0] + sum(len(places) for places in relative)
    return pl.pallas_call(
        functools.partial(steps_kernel, rows, cols, counts, split, relative),
        out_shape=(
            jax.ShapeDtypeStruct((feats, rows * cols), jnp.float32),
            jax.ShapeDtypeStruct((feats, chans), jnp.float32),
        ),
        in_specs=[smem, smem]
        + [pl.BlockSpec(memory_space=pl.ANY)] * len(sources)
        + [vmem] * 8,
        out_specs=(vmem, vmem),
        scratch_shapes=[
            pltpu.VMEM((9 * chans, chans), jnp.bfloat16),
            pltpu.VMEM((3 * chans, chans), jnp.bfloat16),
            pltpu.VMEM((chans, chans), jnp.bfloat16),
            pltpu.VMEM((chans, chans), jnp.bfloat16),
            pltpu.VMEM((tall_rows // 2, 2, cols, chans), jnp.float32),
            pltpu.VMEM((tall_rows // 2 + 1, 2, cols, 3 * chans), jnp.bfloat16),
            pltpu.VMEM((feats, tall_rows * cols), jnp.float32),
            pltpu.SemaphoreType.DMA((3, most)),
        ],
        compiler_params=pltpu.CompilerParams(vmem_limit_bytes=52 * 2**20),
        cost_estimate=pl.CostEstimate(
            flops=2 * token_rows * chans * chans * 12,
            bytes_accessed=12 * chans * chans * 2,
            transcendentals=4 * token_rows * chans,
        ),
    )(flags, factors, *sources, x, noise, key_blocks, value_blocks, bias, gains, w_in, w_final)


def advantages(onehot, own, rewards, own_reward):
    counts = jnp.sum(onehot, axis=0)
    sums = jnp.sum(onehot * rewards[:, None], axis=0)
    squares = jnp.sum(onehot * (rewards * rewards)[:, None], axis=0)
    safe_count = jnp.maximum(counts, 1.0)
    means = sums / safe_count
    spreads = jnp.sqrt(jnp.maximum(squares / safe_count - means * means, 1.0))
    own_mean = jnp.sum(own * means)
    own_spread = jnp.sum(own * spreads)
    return (own_reward - own_mean) / own_spread


def per_device(
    latents,
    noise,
    rewards,
    prompt_ids,
    context,
    time_bias,
    gain_first,
    gain_second,
    gain_third,
    w_in,
    w_conv,
    w_query,
    w_key,
    w_value,
    w_attn_out,
    w_final,
    moment_first,
    moment_second,
):
    sec_count = lax.axis_size("sec")
    dev_count = lax.axis_size("dev")
    prompt_count, context_tokens, _ = context.shape
    assert latents.shape[0] == 1
    col_piece = w_conv.shape[1]
    chans = col_piece * dev_count
    feats = w_in.shape[0] * sec_count
    rows, cols = latents.shape[2] // 2, latents.shape[3] // 2

    pieces = [
        w_conv,
        w_query,
        w_attn_out,
        w_in,
        w_final.astype(jnp.bfloat16).reshape(-1, col_piece),
    ]
    counts = [piece.shape[0] for piece in pieces]
    big = counts[:3]
    used = sum(counts)
    unit = 16 * dev_count
    padded = -(-used // unit) * unit
    whole_tiles = all(count % 16 == 0 for count in big)
    split = counts[0]
    pieces.append(jnp.zeros((padded - used, col_piece), jnp.bfloat16))
    block = jnp.concatenate(pieces, axis=0)
    block = lax.all_to_all(block, "dev", split_axis=0, concat_axis=1, tiled=True)
    packed = lax.all_gather(block, ("sec", "dev"), axis=0, tiled=True)
    packed = packed.reshape(sec_count, padded, chans)
    sources, relative = [packed], []
    at = split + counts[1] + counts[2]
    in_full = packed[:, at : at + counts[3]].reshape(feats, chans)
    at += counts[3]
    final_full = (
        packed[:, at : at + counts[4]]
        .reshape(sec_count, counts[4], dev_count, col_piece)
        .transpose(0, 2, 1, 3)
        .reshape(sec_count, dev_count, chans // sec_count, feats // dev_count)
        .transpose(0, 2, 1, 3)
        .reshape(chans, feats)
    )
    if not whole_tiles:
        first = [sum(big[:k]) for k in range(3)]
        sources = [
            jnp.concatenate(
                [packed[:, f : f + c].reshape(-1, chans) for f, c in zip(first, big)], axis=0
            )[None]
        ]
        big = [count * sec_count for count in big]
        split = big[0]

    both = jnp.stack([rewards, prompt_ids.astype(jnp.float32)], axis=1)
    both = doubled_gather(both, "sec")
    all_rewards = both[:, 0]
    catalog = jnp.arange(prompt_count, dtype=jnp.int32)
    onehot = (both[:, 1].astype(jnp.int32)[:, None] == catalog[None, :]).astype(jnp.float32)
    own = (prompt_ids == catalog).astype(jnp.float32)
    advantage = advantages(onehot, own, all_rewards, rewards[0])

    key_rows = w_key.shape[0]
    tokens_up = -(-context_tokens // 16) * 16
    own_context = lax.dynamic_slice_in_dim(
        context, lax.axis_index("sec") * key_rows, key_rows, axis=2
    )
    own_context = jnp.pad(own_context, ((0, 0), (0, tokens_up - context_tokens), (0, 0)))
    partial = jnp.dot(
        own_context.reshape(prompt_count * tokens_up, key_rows),
        jnp.concatenate([w_key, w_value], axis=1),
        preferred_element_type=jnp.float32,
    ).reshape(prompt_count, tokens_up, 2 * col_piece)
    wanted = jnp.einsum(
        "ip,ptc->itc", onehot, partial, precision=lax.Precision.HIGHEST
    ).astype(jnp.bfloat16)
    arrived = lax.all_to_all(wanted, "sec", split_axis=0, concat_axis=0, tiled=True)
    own_part = jnp.sum(arrived.astype(jnp.float32), axis=0, keepdims=True).astype(jnp.bfloat16)
    whole = doubled_gather(own_part, "dev").reshape(dev_count, tokens_up, 2, col_piece)
    whole = whole.transpose(2, 1, 0, 3).reshape(2, tokens_up, chans)
    lane = 2 * HEAD
    pairs = chans // lane
    valid = jnp.arange(tokens_up)[None, :, None] < context_tokens
    by_pair = jnp.where(valid, whole, 0).reshape(2, tokens_up, pairs, 2, HEAD)
    by_pair = jnp.pad(by_pair, ((0, 0), (0, lane - tokens_up), (0, 0), (0, 0), (0, 0)))
    eye = jnp.eye(2, dtype=jnp.bfloat16)
    key_blocks = (
        (by_pair[0] * (1.0 / math.sqrt(HEAD))).astype(jnp.bfloat16).transpose(1, 2, 3, 0)[
            :, :, :, None, :
        ]
        * eye[None, :, None, :, None]
    ).reshape(pairs, lane, 2 * lane)
    value_blocks = (
        by_pair[1].transpose(1, 2, 0, 3)[:, :, :, None, :] * eye[None, :, None, :, None]
    ).reshape(pairs, 2 * lane, lane)
    inside = (jnp.arange(lane) < context_tokens).astype(jnp.bfloat16)
    ones = jnp.broadcast_to(
        inside[None, :, None, None] * eye[:, None, :, None], (2, lane, 2, HEAD)
    ).reshape(1, 2 * lane, lane)
    value_blocks = jnp.concatenate(
        [value_blocks, jnp.broadcast_to(ones, value_blocks.shape)], axis=2
    )

    position = lax.axis_index("dev")
    flags = [position > 0, position < dev_count - 1, lax.axis_index("sec"), position]
    planes = jnp.concatenate([latents, noise[:, 0]], axis=0)
    planes = to_tokens(with_halo(planes, "dev", 2, 2 * HALO))
    x, noise_wide = planes[0], planes[1:]
    plans = [plan(k) for k in range(STEPS)]
    factors = jnp.array([(s, b, g, b / g) for s, b, g in plans], jnp.float32)

    gains = jnp.stack([0.5 * gain_first, gain_second, 0.5 * gain_third])
    rest = (key_blocks, value_blocks, gains, in_full, final_full)
    gradient = jnp.zeros((feats, chans), jnp.float32)
    for first in range(0, STEPS, GROUP):
        if first:
            x = with_halo(x, "dev", 1, HALO * cols)
        part = slice(first, first + GROUP)
        x, share = run_steps(
            rows,
            cols,
            big,
            split,
            relative,
            jnp.stack([jnp.int32(flag) for flag in flags + [first]]),
            factors[part],
            sources,
            x,
            noise_wide,
            rest,
            time_bias[part],
        )
        gradient = gradient + share
    latent = from_tokens(x, rows, cols)[None]

    gradient = gradient * advantage
    row_piece = chans // sec_count
    arranged = gradient.reshape(dev_count, feats // dev_count, sec_count, row_piece)
    arranged = arranged.transpose(2, 0, 1, 3).reshape(sec_count * dev_count, -1)
    arrived = lax.all_to_all(arranged, ("sec", "dev"), split_axis=0, concat_axis=0, tiled=True)
    grad_shard = jnp.sum(arrived, axis=0).reshape(feats // dev_count, row_piece).T
    grad_shard = -grad_shard / sec_count
    moment_one = 0.9 * moment_first + 0.1 * grad_shard
    moment_two = 0.999 * moment_second + 0.001 * grad_shard * grad_shard
    new_weight = w_final - learn_rate * moment_one / (jnp.sqrt(moment_two) + 1e-08)
    return (latent, new_weight, moment_one, moment_two)


def solution(mesh):
    weight = P("sec", "dev")
    placed = (
        (P("sec", None, "dev", None), P(None, "sec", None, "dev", None), P("sec"), P("sec"))
        + (P(),) * 5
        + (weight,) * 9
    )
    return jax.shard_map(
        per_device,
        mesh=mesh,
        in_specs=placed,
        out_specs=(P("sec", None, "dev", None), weight, weight, weight),
        check_vma=False,
    )
```
